512 devices in a mesh: gx: 8 (over x, core), gy: 4 (over y), gz: 16 (over z).
Axes of the slice: x: 4, y: 4, z: 16, core: 2. Of those that a mesh axis runs over, the one named last changes fastest.
Arguments:
- rhs: bfloat16 [16, 524288], P(None, ('gx', 'gy', 'gz')), may hold values from -6 to 6
- leaf_basis: bfloat16 [2048, 64, 256], P(('gx', 'gy', 'gz')), may hold values from -0.375 to 0.375
- leaf_transfer: bfloat16 [2048, 64, 64], P(('gx', 'gy', 'gz')), may hold values from -0.375 to 0.375
- leaf_coupling: bfloat16 [2048, 6, 64, 64], P(('gx', 'gy', 'gz')), may hold values from -0.3125 to 0.3125
- coupling_sources: int32 [2048, 6], P(('gx', 'gy', 'gz')), may hold values from -1 to 2047, as said below
- near_tiles: bfloat16 [2048, 3, 256, 256], P(('gx', 'gy', 'gz')), may hold values from -0.21875 to 0.21875
- near_sources: int32 [2048, 3], P(('gx', 'gy', 'gz')), may hold values from -1 to 2047, as said below
- top_transfer: bfloat16 [4, 2, 64, 64], replicated, may hold values from -0.625 to 0.625
- cluster_coupling: bfloat16 [5, 2, 64, 64], replicated, may hold values from -0.5 to 0.5
Outputs:
- product: bfloat16 [16, 524288], P(None, ('gx', 'gy', 'gz'))
The draws below stay inside these ranges and needn't reach their ends.
Inputs may be any that keep to these rules, and one draw needn't show every extreme that they name: `near_sources`: slot 0 of each leaf is the leaf itself; every other entry is -1 (no block) or a leaf at most 2 places from its target leaf in the global order. `coupling_sources`: each entry is -1 (no block) or a leaf other than the target, at most 2 places from it in the global order.
All inputs are finite; a program needn't handle non-finite values.
Results may differ from the reference program's by a relative error of at most 0.0043.
Values may be sent and summed in bfloat16 or wider, within the bound.
No kernel may reach another device: no remote copies, remote signals or barrier semaphores. Data moves between devices by JAX's collectives and lax.ppermute only.
A program may use at most 64 MiB of HBM per device.

```python
import jax
import jax.numpy as jnp
from jax import lax

LEAF = 256
RANK = 64
NRHS = 16
NEAR = 3
ADM = 6
TOPL = 4
LEAF_DEV = 4
REACH = 2
LEAVES = 2048
UNKNOWNS = 524288
DEVICES = 512


def local_sources(key, slots, first_self):
    offset_key, keep_key = jax.random.split(key)
    target = jnp.arange(LEAVES, dtype=jnp.int32)[:, None]
    if first_self:
        offset = jax.random.randint(offset_key, (LEAVES, slots), -REACH, REACH + 1)
    else:
        offset = jax.random.randint(offset_key, (LEAVES, slots), -REACH, REACH)
        offset = jnp.where(offset >= 0, offset + 1, offset)
    source = target + offset.astype(jnp.int32)
    keep_slot = jax.random.randint(keep_key, (LEAVES, slots), 0, 4) > 0
    inside = (source >= 0) & (source < LEAVES)
    source = jnp.where(keep_slot & inside, source, -1)
    if first_self:
        source = source.at[:, 0].set(target[:, 0])
        after_slot = 1
        before_slot = 2
    else:
        after_slot = 0
        before_slot = 1
    leaf_pos = target[:, 0] % LEAF_DEV
    after_leaf = target[:, 0] + 1
    before_leaf = target[:, 0] - 1
    need_after = (leaf_pos == LEAF_DEV - 1) & (after_leaf < LEAVES)
    need_before = (leaf_pos == 0) & (before_leaf >= 0)
    source = source.at[:, after_slot].set(jnp.where(need_after, after_leaf, source[:, after_slot]))
    source = source.at[:, before_slot].set(jnp.where(need_before, before_leaf, source[:, before_slot]))
    source = source.at[0, slots - 1].set(-1)
    return source.astype(jnp.int32)


def draw_near_sources(key, part):
    key = jax.random.fold_in(key, 11)
    return local_sources(key, NEAR, True)


def draw_coupling_sources(key, part):
    key = jax.random.fold_in(key, 12)
    return local_sources(key, ADM, False)


def shard_levels(key, shape, cuts, smallest, top_value):
    level = 1.0
    for dim, blocks in cuts:
        steps = jax.random.uniform(jax.random.fold_in(jax.random.fold_in(key, 6), dim), (blocks,), jnp.float32, smallest / len(cuts), top_value / len(cuts))
        level = level * jnp.repeat(jnp.exp(steps), shape[dim] // blocks).reshape((-1,) + (1,) * (len(shape) - 1 - dim))
    return level


def bell_draw(key, extent, scale, limit, cuts=(), kind=jnp.bfloat16):
    values = scale * jax.random.normal(key, extent, jnp.float32)
    if cuts:
        values = values * shard_levels(key, extent, cuts, -0.22, 0.18)
    return jnp.clip(values, -limit, limit).astype(kind)


def setup_inputs(seed: int = 0) -> dict:
    seeds = jax.random.split(jax.random.key(seed), 10)
    rhs = bell_draw(seeds[0], (NRHS, UNKNOWNS), 1.0, 6.0, ((1, 512),))
    leaf_basis = bell_draw(seeds[1], (LEAVES, RANK, LEAF), LEAF ** -0.5, 0.375, ((0, 512),))
    leaf_transfer = bell_draw(seeds[2], (LEAVES, RANK, RANK), (RANK * LEAF_DEV) ** -0.5, 0.375, ((0, 512),))
    leaf_coupling = bell_draw(seeds[3], (LEAVES, ADM, RANK, RANK), (RANK * ADM) ** -0.5, 0.3125, ((0, 512),))
    coupling_sources = draw_coupling_sources(jax.random.fold_in(seeds[9], 71), 0)
    near_tiles = bell_draw(seeds[5], (LEAVES, NEAR, LEAF, LEAF), (LEAF * NEAR) ** -0.5, 0.21875, ((0, 512),))
    near_sources = draw_near_sources(jax.random.fold_in(seeds[9], 71), 0)
    top_transfer = bell_draw(seeds[7], (TOPL, 2, RANK, RANK), (RANK * 3 // 2) ** -0.5, 0.625)
    cluster_coupling = bell_draw(seeds[8], (TOPL + 1, 2, RANK, RANK), (2 * RANK) ** -0.5, 0.5)
    return {"rhs": rhs, "leaf_basis": leaf_basis, "leaf_transfer": leaf_transfer, "leaf_coupling": leaf_coupling, "coupling_sources": coupling_sources, "near_tiles": near_tiles, "near_sources": near_sources, "top_transfer": top_transfer, "cluster_coupling": cluster_coupling}


def reference(rhs, leaf_basis, leaf_transfer, leaf_coupling, coupling_sources, near_tiles, near_sources, top_transfer, cluster_coupling):
    exact = lax.Precision.HIGHEST
    blocks = rhs.reshape(NRHS, LEAVES, LEAF)
    coeffs = jnp.einsum('rts,tks->trk', blocks.astype(jnp.float32), leaf_basis.astype(jnp.float32), precision=exact).astype(jnp.bfloat16)
    usable = coupling_sources >= 0
    picked = coeffs[jnp.clip(coupling_sources, 0, LEAVES - 1).astype(jnp.int32)]
    picked = jnp.where(usable[:, :, None, None], picked, jnp.zeros((), jnp.bfloat16))
    leaf_field = jnp.einsum('tark,takm->trm', picked.astype(jnp.float32), leaf_coupling.astype(jnp.float32), precision=exact)
    grouped = coeffs.reshape(DEVICES, LEAF_DEV, NRHS, RANK).astype(jnp.float32)
    leaf_mats = leaf_transfer.reshape(DEVICES, LEAF_DEV, RANK, RANK).astype(jnp.float32)
    device_level = jnp.einsum('dlrk,dlkm->drm', grouped, leaf_mats, precision=exact)
    up_mats = top_transfer.astype(jnp.float32)
    coupling_mats = cluster_coupling.astype(jnp.float32)
    climbed = [device_level]
    for height in range(TOPL):
        before = climbed[-1]
        pairs = before.reshape(before.shape[0] // 2, 2, NRHS, RANK)
        climbed.append(jnp.einsum('gprk,pkm->grm', pairs, up_mats[height], precision=exact))
    fields = []
    for height in range(TOPL + 1):
        values = climbed[height]
        zero_row = jnp.zeros_like(values[:1])
        lower_side = jnp.concatenate([zero_row, values[:-1]], 0)
        upper_side = jnp.concatenate([values[1:], zero_row], 0)
        fields.append(jnp.einsum('grk,km->grm', lower_side, coupling_mats[height, 0], precision=exact)
                      + jnp.einsum('grk,km->grm', upper_side, coupling_mats[height, 1], precision=exact))
    incoming = fields[TOPL]
    for height in range(TOPL, 0, -1):
        lowered = jnp.einsum('grm,pkm->gprk', incoming, up_mats[height - 1], precision=exact)
        incoming = fields[height - 1] + lowered.reshape(-1, NRHS, RANK)
    spread = jnp.einsum('drm,dlkm->dlrk', incoming, leaf_mats, precision=exact).reshape(LEAVES, NRHS, RANK)
    potential = (leaf_field + spread).astype(jnp.bfloat16)
    far_part = jnp.einsum('trk,tks->rts', potential.astype(jnp.float32), leaf_basis.astype(jnp.float32), precision=exact)

    def near_block(operands):
        tiles, sources = operands
        fetched = jnp.take(blocks, jnp.clip(sources, 0, LEAVES - 1).astype(jnp.int32), axis=1)
        fetched = jnp.where((sources >= 0)[None, :, :, None], fetched, jnp.zeros((), jnp.bfloat16))
        return jnp.einsum('rtns,tnsu->tru', fetched.astype(jnp.float32), tiles.astype(jnp.float32), precision=exact)

    near_part = lax.map(near_block, (near_tiles.reshape(DEVICES, LEAF_DEV, NEAR, LEAF, LEAF),
                                     near_sources.reshape(DEVICES, LEAF_DEV, NEAR)))
    near_part = near_part.reshape(LEAVES, NRHS, LEAF).transpose(1, 0, 2)
    return (far_part + near_part).reshape(NRHS, UNKNOWNS).astype(jnp.bfloat16)
```

```python
import jax
import jax.numpy as jnp
from jax import lax
from jax.experimental import pallas as pl
from jax.experimental.pallas import tpu as pltpu
from jax.sharding import PartitionSpec as P

LEAF = 256
RANK = 64
NRHS = 16
NEAR = 3
ADM = 6
TOPL = 4
LEAF_DEV = 4
REACH = 2
LINE = 16
LEADER = 11
AXES = ("gx", "gy", "gz")
EDGE = REACH * (LEAF + RANK)
VMEM = pl.BlockSpec(memory_space=pltpu.VMEM)
SMEM = pl.BlockSpec(memory_space=pltpu.SMEM)
HBM = pl.BlockSpec(memory_space=pltpu.HBM)
STAGED = 9
NT = (((1,), (1,)), ((), ()))
NN = (((1,), (0,)), ((), ()))


def dot(a, b, dims=NN):
    return lax.dot_general(a, b, dims, preferred_element_type=jnp.float32)


def dot_split(a, b, dims=NN):
    high = a.astype(jnp.bfloat16)
    low = (a - high.astype(jnp.float32)).astype(jnp.bfloat16)
    both = dot(jnp.concatenate([high, low], 0), b, dims)
    return both[: a.shape[0]] + both[a.shape[0] :]


def coeff_kernel(*refs):
    staged, coeffs_ref, sends_ref, tail_ref, head_ref = refs[:STAGED], *refs[STAGED : STAGED + 4]
    kept, done = refs[STAGED + 4 : -1], refs[-1]
    copies = [
        pltpu.make_async_copy(staged[i], kept[i], done.at[i]) for i in range(STAGED)
    ]
    for copy in copies:
        copy.start()
    rhs_ref, basis_ref, transfer_ref = kept[:3]
    copies[0].wait()
    wide = REACH * LEAF
    tail_ref[:, :wide] = rhs_ref[:, (LEAF_DEV - REACH) * LEAF :]
    head_ref[:, :wide] = rhs_ref[:, :wide]
    copies[1].wait()
    parts = []
    for t in range(LEAF_DEV):
        block = rhs_ref[:, t * LEAF : (t + 1) * LEAF]
        parts.append(dot(block, basis_ref[t], NT).astype(jnp.bfloat16))
    copies[2].wait()
    root = dot(parts[0], transfer_ref[0])
    for t in range(1, LEAF_DEV):
        root = root + dot(parts[t], transfer_ref[t])
    packed = jnp.concatenate([root[:8], root[8:]], 1)
    for j in range(LINE):
        sends_ref[8 * j : 8 * (j + 1), :] = packed
    coeffs = jnp.concatenate(parts, 1)
    coeffs_ref[...] = coeffs
    tail_ref[:, wide:] = coeffs[:, (LEAF_DEV - REACH) * RANK :]
    head_ref[:, wide:] = coeffs[:, : REACH * RANK]
    for copy in copies[3:]:
        copy.wait()


def near_kernel(
    near_src, coup_src, rhs_ref, coeffs_ref, lower_ref, upper_ref, tiles_ref, coupling_ref,
    near_ref, field_ref, blocks, leaf_coeffs,
):
    own = near_src[0, 0]
    anchor = own - REACH
    none = LEAF_DEV + 2 * REACH
    wide = REACH * LEAF
    for i in range(REACH):
        blocks[i] = lower_ref[:, i * LEAF : (i + 1) * LEAF]
        blocks[REACH + LEAF_DEV + i] = upper_ref[:, i * LEAF : (i + 1) * LEAF]
        leaf_coeffs[i] = lower_ref[:, wide + i * RANK : wide + (i + 1) * RANK]
        leaf_coeffs[REACH + LEAF_DEV + i] = upper_ref[:, wide + i * RANK : wide + (i + 1) * RANK]
    for t in range(LEAF_DEV):
        blocks[REACH + t] = rhs_ref[:, t * LEAF : (t + 1) * LEAF]
        leaf_coeffs[REACH + t] = coeffs_ref[:, t * RANK : (t + 1) * RANK]
    blocks[none] = jnp.zeros((NRHS, LEAF), jnp.bfloat16)
    leaf_coeffs[none] = jnp.zeros((NRHS, RANK), jnp.bfloat16)

    def place(source):
        return jnp.where(source >= 0, jnp.clip(source - anchor, 0, none - 1), none)

    fields = []
    for t in range(LEAF_DEV):
        picked = jnp.concatenate([blocks[place(near_src[t, n])] for n in range(NEAR)], 1)
        near_ref[:, t * LEAF : (t + 1) * LEAF] = dot(picked, tiles_ref[t].reshape(NEAR * LEAF, LEAF))
        taken = jnp.concatenate([leaf_coeffs[place(coup_src[t, a])] for a in range(ADM)], 1)
        fields.append(dot(taken, coupling_ref[t].reshape(ADM * RANK, RANK)))
    field_ref[...] = jnp.concatenate(fields, 1)


def tree_kernel(got_ref, up_ref, coup_ref, own_ref, after_ref, before_ref, *levels):
    place = lax.axis_index("gz")
    wide = got_ref[...].reshape(LINE, 8, 2 * RANK)
    order = [(z - LEADER) % LINE for z in range(LINE)]
    for z in range(LINE):
        levels[0][0, z] = wide[order[z], :, :RANK]
        levels[0][1, z] = wide[order[z], :, RANK:]
    for h in range(1, TOPL + 1):
        count = LINE >> h
        before = levels[h - 1][...].reshape(2, count, 2, 8, RANK)
        pairs = jnp.concatenate([before[:, :, 0], before[:, :, 1]], -1)
        mat = up_ref[h - 1].reshape(2 * RANK, RANK)
        levels[h][...] = dot_split(pairs.reshape(NRHS * count, 2 * RANK), mat).reshape(2, count, 8, RANK)

    def cluster(h, q):
        return levels[h][:, q].reshape(NRHS, RANK)

    zero = jnp.zeros((NRHS, RANK), jnp.float32)
    fields = []
    for h in range(TOPL + 1):
        count = LINE >> h
        q = place >> h
        if h < TOPL:
            lower = cluster(h, jnp.maximum(q - 1, 0)) * (q > 0).astype(jnp.float32)
            upper = cluster(h, jnp.minimum(q + 1, count - 1)) * (q < count - 1).astype(jnp.float32)
        else:
            lower = upper = zero
        last = cluster(h, count - 1) * (q == 0).astype(jnp.float32)
        first = cluster(h, 0) * (q == count - 1).astype(jnp.float32)
        sides = jnp.concatenate(
            [
                jnp.concatenate([lower, upper], 1),
                jnp.concatenate([last, zero], 1),
                jnp.concatenate([zero, first], 1),
            ],
            0,
        )
        fields.append(dot_split(sides, coup_ref[h].reshape(2 * RANK, RANK)))
    incoming = fields[TOPL]
    for h in range(TOPL, 0, -1):
        parity = (place >> (h - 1)) & 1
        incoming = fields[h - 1] + dot_split(incoming, up_ref[h - 1, parity], NT)
    own_ref[...] = incoming[:NRHS]
    after_ref[...] = incoming[NRHS : 2 * NRHS]
    before_ref[...] = incoming[2 * NRHS :]


def out_kernel(own_ref, lower_ref, upper_ref, field_ref, near_ref, transfer_ref, basis_ref, out_ref):
    incoming = own_ref[...] + lower_ref[...] + upper_ref[...]
    spread = dot_split(incoming, transfer_ref[...].reshape(LEAF_DEV * RANK, RANK), NT)
    potential = (field_ref[...] + spread).astype(jnp.bfloat16)
    for t in range(LEAF_DEV):
        far = dot(potential[:, t * RANK : (t + 1) * RANK], basis_ref[t])
        at = slice(t * LEAF, (t + 1) * LEAF)
        out_ref[:, at] = (far + near_ref[:, at]).astype(jnp.bfloat16)


def shifted(values, count, distance):
    route = [(i, i + distance) for i in range(count) if 0 <= i + distance < count]
    return lax.ppermute(values, AXES, route)


def call(kernel, outs, scratch=(), ins=(), flops=0, moved=0, name=None):
    return pl.pallas_call(
        kernel,
        out_shape=[jax.ShapeDtypeStruct(shape, dtype) for shape, dtype in outs],
        in_specs=list(ins),
        out_specs=[VMEM] * len(outs),
        scratch_shapes=list(scratch),
        cost_estimate=pl.CostEstimate(flops=flops, bytes_accessed=moved, transcendentals=0),
        compiler_params=pltpu.CompilerParams(vmem_limit_bytes=24 * 2**20),
        name=name,
    )


def local(
    rhs,
    leaf_basis,
    leaf_transfer,
    leaf_coupling,
    coupling_sources,
    near_tiles,
    near_sources,
    top_transfer,
    cluster_coupling,
):
    bf16, f32 = jnp.bfloat16, jnp.float32
    count = lax.axis_size(AXES)
    width = LEAF_DEV * LEAF
    ranks = LEAF_DEV * RANK
    inputs = (
        rhs, leaf_basis, leaf_transfer, top_transfer, cluster_coupling,
        near_sources, coupling_sources, leaf_coupling, near_tiles,
    )
    inputs = [pltpu.with_memory_space_constraint(x, pltpu.HBM) for x in inputs]
    coeffs, sends, tail, head, *kept = call(
        coeff_kernel,
        [
            ((NRHS, ranks), bf16),
            ((LINE * 8, 2 * RANK), f32),
            ((NRHS, EDGE), bf16),
            ((NRHS, EDGE), bf16),
        ]
        + [(x.shape, x.dtype) for x in inputs],
        scratch=[pltpu.SemaphoreType.DMA((STAGED,))],
        ins=[HBM] * STAGED,
        flops=2 * NRHS * ranks * (LEAF + RANK),
        moved=2**21,
        name="coeffs",
    )(*inputs)
    rhs, leaf_basis, leaf_transfer, top_transfer, cluster_coupling = kept[:5]
    near_sources, coupling_sources, leaf_coupling, near_tiles = kept[5:]
    ring = [(LEADER + i) % LINE for i in range(LINE)]
    got = lax.all_to_all(sends, "gz", 0, 0, tiled=True, axis_index_groups=[ring])
    lower = shifted(tail, count, 1)
    upper = shifted(head, count, -1)
    near, field = call(
        near_kernel,
        [((NRHS, width), f32), ((NRHS, ranks), f32)],
        scratch=[
            pltpu.VMEM((LEAF_DEV + 2 * REACH + 1, NRHS, LEAF), bf16),
            pltpu.VMEM((LEAF_DEV + 2 * REACH + 1, NRHS, RANK), bf16),
        ],
        ins=[SMEM, SMEM] + [VMEM] * 6,
        flops=2 * NRHS * LEAF_DEV * (NEAR * LEAF * LEAF + ADM * RANK * RANK),
        moved=2**21,
        name="near",
    )(near_sources, coupling_sources, rhs, coeffs, lower, upper, near_tiles, leaf_coupling)
    own, after, before = call(
        tree_kernel,
        [((NRHS, RANK), f32)] * 3,
        scratch=[pltpu.VMEM((2, LINE >> h, 8, RANK), f32) for h in range(TOPL + 1)],
        ins=[VMEM] * 3,
        flops=2**23,
        moved=2**18,
        name="tree",
    )(got, top_transfer, cluster_coupling)
    from_lower = shifted(after, count, LINE)
    from_upper = shifted(before, count, -LINE)
    return call(
        out_kernel,
        [((NRHS, width), bf16)],
        ins=[VMEM] * 7,
        flops=2 * NRHS * ranks * (LEAF + RANK),
        moved=2**18,
        name="out",
    )(own, from_lower, from_upper, field, near, leaf_transfer, leaf_basis)[0]


def solution(mesh):
    placed = (
        P(None, AXES),
        P(AXES, None, None),
        P(AXES, None, None),
        P(AXES, None, None, None),
        P(AXES, None),
        P(AXES, None, None, None),
        P(AXES, None),
        P(),
        P(),
    )
    return jax.shard_map(
        local, mesh=mesh, in_specs=placed, out_specs=P(None, AXES), check_vma=False
    )
```

```python
import jax
import jax.numpy as jnp
from jax import lax
from jax.experimental import pallas as pl
from jax.experimental.pallas import tpu as pltpu
from jax.sharding import PartitionSpec as P

LEAF = 256
RANK = 64
NRHS = 16
NEAR = 3
ADM = 6
TOPL = 4
LEAF_DEV = 4
REACH = 2
LINE = 16
PAIR = 2 * LINE
LEADER = 11
MEMBERS = [(1, LEADER), (0, LEADER)] + [(line, z) for z in [12, 10, 9, 8, 7, 6, 5, 4, 3, 2, 1, 0, 15, 14, 13] for line in range(2)]
AXES = ("gx", "gy", "gz")
EDGE = REACH * (LEAF + RANK)
VMEM = pl.BlockSpec(memory_space=pltpu.VMEM)
SMEM = pl.BlockSpec(memory_space=pltpu.SMEM)
HBM = pl.BlockSpec(memory_space=pltpu.HBM)
STAGED = 7
HELD = 2
EARLY = 6
NT = (((1,), (1,)), ((), ()))
NN = (((1,), (0,)), ((), ()))


def dot(a, b, dims=NN):
    return lax.dot_general(a, b, dims, preferred_element_type=jnp.float32)


def dot_split(a, b, dims=NN):
    high = a.astype(jnp.bfloat16)
    low = (a - high.astype(jnp.float32)).astype(jnp.bfloat16)
    both = dot(jnp.concatenate([high, low], 0), b, dims)
    return both[: a.shape[0]] + both[a.shape[0] :]


def hold(staged, kept, done):
    return [pltpu.make_async_copy(staged[i], kept[i], done.at[i]) for i in range(HELD)]


def coeff_kernel(*refs):
    count = STAGED + HELD
    staged, coeffs_ref, sends_ref, head_ref, tail_ref = refs[:count], *refs[count : count + 4]
    kept, done, held = refs[count + 4 : -2], refs[-2], refs[-1]
    copies = [
        pltpu.make_async_copy(staged[i], kept[i], done.at[i]) for i in range(STAGED)
    ]
    for copy in copies:
        copy.start()
    early = lax.axis_index("gz") < EARLY

    @pl.when(early)
    def _():
        for copy in hold(staged[STAGED:], kept[STAGED:], held):
            copy.start()

    rhs_ref, basis_ref, transfer_ref = kept[:3]
    copies[0].wait()
    wide = REACH * LEAF
    tail_ref[:, :wide] = rhs_ref[:, (LEAF_DEV - REACH) * LEAF :]
    head_ref[:, :wide] = rhs_ref[:, :wide]
    copies[1].wait()
    parts = []
    for t in range(LEAF_DEV):
        block = rhs_ref[:, t * LEAF : (t + 1) * LEAF]
        parts.append(dot(block, basis_ref[t], NT).astype(jnp.bfloat16))
    copies[2].wait()
    root = dot(parts[0], transfer_ref[0])
    for t in range(1, LEAF_DEV):
        root = root + dot(parts[t], transfer_ref[t])
    packed = jnp.concatenate([root[:8], root[8:]], 1)
    packed = jnp.concatenate([packed, packed], 0).astype(jnp.bfloat16)
    for j in range(PAIR // 2):
        sends_ref[16 * j : 16 * (j + 1), :] = packed
    coeffs = jnp.concatenate(parts, 1)
    coeffs_ref[...] = coeffs
    tail_ref[:, wide:] = coeffs[:, (LEAF_DEV - REACH) * RANK :]
    head_ref[:, wide:] = coeffs[:, : REACH * RANK]
    for copy in copies[3:]:
        copy.wait()

    @pl.when(early)
    def _():
        for copy in hold(staged[STAGED:], kept[STAGED:], held):
            copy.wait()


def near_kernel(
    near_src, coup_src, rhs_ref, coeffs_ref, upper_ref, lower_ref, coupling_hbm, tiles_hbm,
    coupling_in, tiles_in, near_ref, field_ref, coupling_ref, tiles_ref, blocks, leaf_coeffs, held,
):
    late = lax.axis_index("gz") >= EARLY

    @pl.when(late)
    def _():
        for copy in hold([coupling_hbm, tiles_hbm], [coupling_ref, tiles_ref], held):
            copy.start()

    own = near_src[0, 0]
    anchor = own - REACH
    none = LEAF_DEV + 2 * REACH
    wide = REACH * LEAF
    for i in range(REACH):
        blocks[i] = lower_ref[:, i * LEAF : (i + 1) * LEAF]
        blocks[REACH + LEAF_DEV + i] = upper_ref[:, i * LEAF : (i + 1) * LEAF]
        leaf_coeffs[i] = lower_ref[:, wide + i * RANK : wide + (i + 1) * RANK]
        leaf_coeffs[REACH + LEAF_DEV + i] = upper_ref[:, wide + i * RANK : wide + (i + 1) * RANK]
    for t in range(LEAF_DEV):
        blocks[REACH + t] = rhs_ref[:, t * LEAF : (t + 1) * LEAF]
        leaf_coeffs[REACH + t] = coeffs_ref[:, t * RANK : (t + 1) * RANK]
    blocks[none] = jnp.zeros((NRHS, LEAF), jnp.bfloat16)
    leaf_coeffs[none] = jnp.zeros((NRHS, RANK), jnp.bfloat16)

    def place(source):
        return jnp.where(source >= 0, jnp.clip(source - anchor, 0, none - 1), none)

    @pl.when(late)
    def _():
        for copy in hold([coupling_hbm, tiles_hbm], [coupling_ref, tiles_ref], held):
            copy.wait()

    fields = []
    for t in range(LEAF_DEV):
        picked = jnp.concatenate([blocks[place(near_src[t, n])] for n in range(NEAR)], 1)
        near_ref[:, t * LEAF : (t + 1) * LEAF] = dot(picked, tiles_ref[t].reshape(NEAR * LEAF, LEAF))
        taken = jnp.concatenate([leaf_coeffs[place(coup_src[t, a])] for a in range(ADM)], 1)
        fields.append(dot(taken, coupling_ref[t].reshape(ADM * RANK, RANK)))
    field_ref[...] = jnp.concatenate(fields, 1)


def tree_kernel(got_ref, up_ref, coup_ref, own_ref, cross_ref, *levels):
    spot = lax.axis_index("gz")
    half = lax.axis_index("gy") & 1
    place = half * LINE + spot
    wide = got_ref[...].astype(jnp.float32).reshape(PAIR, 8, 2 * RANK)
    for j, (line, z) in enumerate(MEMBERS):
        levels[0][0, line * LINE + z] = wide[j, :, :RANK]
        levels[0][1, line * LINE + z] = wide[j, :, RANK:]
    for h in range(1, TOPL + 1):
        count = PAIR >> h
        before = levels[h - 1][...].reshape(2, count, 2, 8, RANK)
        pairs = jnp.concatenate([before[:, :, 0], before[:, :, 1]], -1)
        mat = up_ref[h - 1].reshape(2 * RANK, RANK)
        levels[h][...] = dot_split(pairs.reshape(NRHS * count, 2 * RANK), mat).reshape(2, count, 8, RANK)

    def cluster(h, q, used):
        return levels[h][:, q].reshape(NRHS, RANK) * used.astype(jnp.float32)

    fields = []
    for h in range(TOPL + 1):
        count = PAIR >> h
        q = place >> h
        low = spot >> h
        sides = [
            cluster(h, jnp.maximum(q - 1, 0), q > 0),
            cluster(h, jnp.minimum(q + 1, count - 1), q < count - 1),
            cluster(h, count - 1, (half == 1) & (low == 0)),
            cluster(h, 0, (half == 0) & (low == (LINE >> h) - 1)),
        ]
        rows = jnp.concatenate([jnp.concatenate(sides[:2], 1), jnp.concatenate(sides[2:], 1)], 0)
        fields.append(dot_split(rows, coup_ref[h].reshape(2 * RANK, RANK)))
    incoming = fields[TOPL]
    for h in range(TOPL, 0, -1):
        parity = (spot >> (h - 1)) & 1
        incoming = fields[h - 1] + dot_split(incoming, up_ref[h - 1, parity], NT)
    own_ref[...] = incoming[:NRHS]
    cross_ref[...] = incoming[NRHS:]


def out_kernel(own_ref, cross_ref, field_ref, near_ref, transfer_ref, basis_ref, out_ref):
    incoming = own_ref[...] + cross_ref[...]
    spread = dot_split(incoming, transfer_ref[...].reshape(LEAF_DEV * RANK, RANK), NT)
    potential = (field_ref[...] + spread).astype(jnp.bfloat16)
    for t in range(LEAF_DEV):
        far = dot(potential[:, t * RANK : (t + 1) * RANK], basis_ref[t])
        at = slice(t * LEAF, (t + 1) * LEAF)
        out_ref[:, at] = (far + near_ref[:, at]).astype(jnp.bfloat16)


def crossed(values, count):
    route = []
    for line in range(1, count // LINE - 1, 2):
        for z in range(LINE):
            low = line * LINE + z
            route += [(low, low + LINE), (low + LINE, low)]
    return lax.ppermute(values, AXES, route)


def shifted(values, count, distance):
    route = [(i, i + distance) for i in range(count) if 0 <= i + distance < count]
    return lax.ppermute(values, AXES, route)


def call(kernel, outs, scratch=(), ins=(), flops=0, moved=0, name=None, aliases=None):
    return pl.pallas_call(
        kernel,
        out_shape=[jax.ShapeDtypeStruct(shape, dtype) for shape, dtype in outs],
        in_specs=list(ins),
        out_specs=[VMEM] * len(outs),
        scratch_shapes=list(scratch),
        cost_estimate=pl.CostEstimate(flops=flops, bytes_accessed=moved, transcendentals=0),
        compiler_params=pltpu.CompilerParams(vmem_limit_bytes=24 * 2**20),
        input_output_aliases=aliases or {},
        name=name,
    )


def local(
    rhs,
    leaf_basis,
    leaf_transfer,
    leaf_coupling,
    coupling_sources,
    near_tiles,
    near_sources,
    top_transfer,
    cluster_coupling,
):
    bf16, f32 = jnp.bfloat16, jnp.float32
    count = lax.axis_size(AXES)
    width = LEAF_DEV * LEAF
    ranks = LEAF_DEV * RANK
    inputs = (
        rhs, leaf_basis, leaf_transfer, top_transfer, cluster_coupling,
        near_sources, coupling_sources, leaf_coupling, near_tiles,
    )
    inputs = [pltpu.with_memory_space_constraint(x, pltpu.HBM) for x in inputs]
    coeffs, sends, head, tail, *kept = call(
        coeff_kernel,
        [
            ((NRHS, ranks), bf16),
            ((PAIR * 8, 2 * RANK), bf16),
            ((NRHS, EDGE), bf16),
            ((NRHS, EDGE), bf16),
        ]
        + [(x.shape, x.dtype) for x in inputs],
        scratch=[pltpu.SemaphoreType.DMA((STAGED,)), pltpu.SemaphoreType.DMA((HELD,))],
        ins=[HBM] * (STAGED + HELD),
        flops=2 * NRHS * ranks * (LEAF + RANK),
        moved=2**21,
        name="coeffs",
    )(*inputs)
    rhs, leaf_basis, leaf_transfer, top_transfer, cluster_coupling = kept[:5]
    near_sources, coupling_sources, coupling_kept, tiles_kept = kept[5:]
    pairs = [
        [(2 * k + line) * LINE + z for line, z in MEMBERS]
        for k in range(lax.axis_size("gy") // 2)
    ]
    got = lax.all_to_all(sends, ("gy", "gz"), 0, 0, tiled=True, axis_index_groups=pairs)
    upper = shifted(head, count, -1)
    lower = shifted(tail, count, 1)
    near, field, _, _ = call(
        near_kernel,
        [((NRHS, width), f32), ((NRHS, ranks), f32)]
        + [(x.shape, x.dtype) for x in (coupling_kept, tiles_kept)],
        scratch=[
            pltpu.VMEM((LEAF_DEV + 2 * REACH + 1, NRHS, LEAF), bf16),
            pltpu.VMEM((LEAF_DEV + 2 * REACH + 1, NRHS, RANK), bf16),
            pltpu.SemaphoreType.DMA((HELD,)),
        ],
        ins=[SMEM, SMEM] + [VMEM] * 4 + [HBM] * 2 + [VMEM] * 2,
        aliases={8: 2, 9: 3},
        flops=2 * NRHS * LEAF_DEV * (NEAR * LEAF * LEAF + ADM * RANK * RANK),
        moved=2**21,
        name="near",
    )(near_sources, coupling_sources, rhs, coeffs, upper, lower, *inputs[-HELD:], coupling_kept, tiles_kept)
    own, cross = call(
        tree_kernel,
        [((NRHS, RANK), f32)] * 2,
        scratch=[pltpu.VMEM((2, PAIR >> h, 8, RANK), f32) for h in range(TOPL + 1)],
        ins=[VMEM] * 3,
        flops=2**23,
        moved=2**18,
        name="tree",
    )(got, top_transfer, cluster_coupling)
    cross = crossed(cross, count)
    return call(
        out_kernel,
        [((NRHS, width), bf16)],
        ins=[VMEM] * 6,
        flops=2 * NRHS * ranks * (LEAF + RANK),
        moved=2**18,
        name="out",
    )(own, cross, field, near, leaf_transfer, leaf_basis)[0]


def solution(mesh):
    placed = (
        P(None, AXES),
        P(AXES, None, None),
        P(AXES, None, None),
        P(AXES, None, None, None),
        P(AXES, None),
        P(AXES, None, None, None),
        P(AXES, None),
        P(),
        P(),
    )
    return jax.shard_map(
        local, mesh=mesh, in_specs=placed, out_specs=P(None, AXES), check_vma=False
    )
```

```python
import jax
import jax.numpy as jnp
from jax import lax
from jax.experimental import pallas as pl
from jax.experimental.pallas import tpu as pltpu
from jax.sharding import PartitionSpec as P

LEAF = 256
RANK = 64
NRHS = 16
NEAR = 3
ADM = 6
TOPL = 4
LEAF_DEV = 4
REACH = 2
LINE = 16
PAIR = 2 * LINE
LEADER = 11
MEMBERS = [(1, LEADER)] + [(line, z) for line in (0, 1) for z in [12, 11, 10, 9, 8, 7, 6, 5, 4, 3, 2, 1, 0, 15, 14, 13] if (line, z) != (1, LEADER)]
AXES = ("gx", "gy", "gz")
EDGE = REACH * (LEAF + RANK)
VMEM = pl.BlockSpec(memory_space=pltpu.VMEM)
SMEM = pl.BlockSpec(memory_space=pltpu.SMEM)
HBM = pl.BlockSpec(memory_space=pltpu.HBM)
STAGED = 5
HELD = 2
EARLY = 6
FOLDED = 4
NT = (((1,), (1,)), ((), ()))
NN = (((1,), (0,)), ((), ()))
TN = (((0,), (0,)), ((), ()))


def dot(a, b, dims=NN):
    return lax.dot_general(a, b, dims, preferred_element_type=jnp.float32)


def dot_split(a, b, dims=NN):
    high = a.astype(jnp.bfloat16)
    low = (a - high.astype(jnp.float32)).astype(jnp.bfloat16)
    both = dot(jnp.concatenate([high, low], 0), b, dims)
    return both[: a.shape[0]] + both[a.shape[0] :]


def dot_wide(a, b, dims=NN):
    high = b.astype(jnp.bfloat16)
    low = (b - high.astype(jnp.float32)).astype(jnp.bfloat16)
    both = dot(a, jnp.concatenate([high, low], 1), dims)
    return both[:, : b.shape[1]] + both[:, b.shape[1] :]


def position():
    spot = lax.axis_index("gz")
    half = lax.axis_index("gy") & 1
    return spot, half, half * LINE + spot


def neighbours(h, spot, half, place):
    count = PAIR >> h
    q, low = place >> h, spot >> h
    return [
        (0, 0, jnp.maximum(q - 1, 0), q > 0),
        (0, 1, jnp.minimum(q + 1, count - 1), q < count - 1),
        (1, 0, count - 1, (half == 1) & (low == 0)),
        (1, 1, 0, (half == 0) & (low == (LINE >> h) - 1)),
    ]


def fold(up_ref, coup_ref, folded_ref, maps):
    spot, half, place = position()
    maps[TOPL][...] = jnp.zeros_like(maps[TOPL])
    down = [None]
    for h in range(1, TOPL + 1):
        step = up_ref[h - 1, (spot >> (h - 1)) & 1]
        down.append(step.T.astype(jnp.float32) if h == 1 else dot_wide(step, down[-1], TN))
    zero = jnp.zeros((RANK, RANK), jnp.float32)
    for h in range(TOPL, -1, -1):
        for to, side, q, used in neighbours(h, spot, half, place):
            mat = coup_ref[h, side]
            term = dot_wide(mat, down[h]) if h else mat.astype(jnp.float32)
            term = term * used.astype(jnp.float32)
            maps[h][q] += jnp.concatenate([zero, term] if to else [term, zero], 1)
        if h:
            mat = up_ref[h - 1].reshape(2 * RANK, RANK)
            for q in range(PAIR >> h):
                maps[h - 1][2 * q : 2 * q + 2] = dot_wide(mat, maps[h][q]).reshape(2, RANK, 2 * RANK)
    for j, (line, z) in enumerate(MEMBERS):
        values = maps[0][line * LINE + z]
        high = values.astype(jnp.bfloat16)
        at = slice(j * RANK, (j + 1) * RANK)
        folded_ref[0, at, :] = high
        folded_ref[1, at, :] = (values - high.astype(jnp.float32)).astype(jnp.bfloat16)


def hold(staged, kept, done):
    return [pltpu.make_async_copy(staged[i], kept[i], done.at[i]) for i in range(HELD)]


def levels_copies(up_hbm, coup_hbm, up_ref, coup_ref, done):
    return [
        pltpu.make_async_copy(up_hbm, up_ref, done.at[0]),
        pltpu.make_async_copy(coup_hbm, coup_ref, done.at[1]),
    ]


def coeff_kernel(*refs):
    count = STAGED + HELD
    staged, (up_hbm, coup_hbm), refs = refs[:count], refs[count : count + 2], refs[count + 2 :]
    coeffs_ref, sends_ref, first_ref, second_ref, folded_ref = refs[:5]
    kept, (done, held, mats), refs = refs[5 : count + 5], refs[count + 5 : count + 8], refs[count + 8 :]
    up_ref, coup_ref, maps = refs[0], refs[1], refs[2:]
    spot = lax.axis_index("gz")
    early, folding = spot < EARLY, spot < FOLDED
    copies = [
        pltpu.make_async_copy(staged[i], kept[i], done.at[i]) for i in range(STAGED)
    ]
    for copy in copies:
        copy.start()

    @pl.when(early)
    def _():
        for copy in hold(staged[STAGED:], kept[STAGED:], held):
            copy.start()

    @pl.when(folding)
    def _():
        for copy in levels_copies(up_hbm, coup_hbm, up_ref, coup_ref, mats):
            copy.start()

    rhs_ref, basis_ref, transfer_ref = kept[:3]
    copies[0].wait()
    copies[1].wait()
    parts = []
    for t in range(LEAF_DEV):
        block = rhs_ref[:, t * LEAF : (t + 1) * LEAF]
        parts.append(dot(block, basis_ref[t], NT).astype(jnp.bfloat16))
    copies[2].wait()
    coeffs = jnp.concatenate(parts, 1)
    root = dot(coeffs, transfer_ref[...].reshape(LEAF_DEV * RANK, RANK))
    packed = jnp.concatenate([root[:8], root[8:]], 1)
    packed = jnp.concatenate([packed, packed], 0).astype(jnp.bfloat16)
    for j in range(PAIR // 2):
        sends_ref[16 * j : 16 * (j + 1), :] = packed
    coeffs_ref[...] = coeffs
    wide = REACH * LEAF
    tail = jnp.concatenate([rhs_ref[:, (LEAF_DEV - REACH) * LEAF :], coeffs[:, (LEAF_DEV - REACH) * RANK :]], 1)
    head = jnp.concatenate([rhs_ref[:, :wide], coeffs[:, : REACH * RANK]], 1)
    odd = jnp.broadcast_to(spot & 1, tail.shape) == 1
    first_ref[...] = jnp.where(odd, tail, head)
    second_ref[...] = jnp.where(odd, head, tail)
    for copy in copies[3:]:
        copy.wait()

    @pl.when(folding)
    def _():
        for copy in levels_copies(up_hbm, coup_hbm, up_ref, coup_ref, mats):
            copy.wait()
        fold(up_ref, coup_ref, folded_ref, maps)

    @pl.when(early)
    def _():
        for copy in hold(staged[STAGED:], kept[STAGED:], held):
            copy.wait()


def near_kernel(
    near_src, coup_src, rhs_ref, coeffs_ref, first_ref, second_ref, coupling_hbm, tiles_hbm,
    coupling_in, tiles_in, near_ref, field_ref, coupling_ref, tiles_ref, blocks, leaf_coeffs, held,
):
    late = lax.axis_index("gz") >= EARLY

    @pl.when(late)
    def _():
        for copy in hold([coupling_hbm, tiles_hbm], [coupling_ref, tiles_ref], held):
            copy.start()

    own = near_src[0, 0]
    anchor = own - REACH
    none = LEAF_DEV + 2 * REACH
    wide = REACH * LEAF
    above = REACH + LEAF_DEV
    odd = lax.axis_index("gz") & 1
    for side_ref, start in ((first_ref, above * odd), (second_ref, above * (1 - odd))):
        for i in range(REACH):
            blocks[start + i] = side_ref[:, i * LEAF : (i + 1) * LEAF]
            leaf_coeffs[start + i] = side_ref[:, wide + i * RANK : wide + (i + 1) * RANK]
    for t in range(LEAF_DEV):
        blocks[REACH + t] = rhs_ref[:, t * LEAF : (t + 1) * LEAF]
        leaf_coeffs[REACH + t] = coeffs_ref[:, t * RANK : (t + 1) * RANK]
    blocks[none] = jnp.zeros((NRHS, LEAF), jnp.bfloat16)
    leaf_coeffs[none] = jnp.zeros((NRHS, RANK), jnp.bfloat16)

    def place(source):
        return jnp.where(source >= 0, jnp.clip(source - anchor, 0, none - 1), none)

    @pl.when(late)
    def _():
        for copy in hold([coupling_hbm, tiles_hbm], [coupling_ref, tiles_ref], held):
            copy.wait()

    fields = []
    for t in range(LEAF_DEV):
        picked = jnp.concatenate([blocks[place(near_src[t, n])] for n in range(NEAR)], 1)
        near_ref[:, t * LEAF : (t + 1) * LEAF] = dot(picked, tiles_ref[t].reshape(NEAR * LEAF, LEAF))
        taken = jnp.concatenate([leaf_coeffs[place(coup_src[t, a])] for a in range(ADM)], 1)
        fields.append(dot(taken, coupling_ref[t].reshape(ADM * RANK, RANK)))
    field_ref[...] = jnp.concatenate(fields, 1)


def tree_kernel(got_ref, folded_ref, up_hbm, coup_hbm, own_ref, cross_ref, up_ref, coup_ref, mats, *levels):
    spot, half, place = position()
    wide = got_ref[...].astype(jnp.float32).reshape(PAIR, 8, 2 * RANK)

    @pl.when(spot < FOLDED)
    def _():
        parts = []
        for j in range(0, PAIR, 2):
            top = jnp.concatenate([wide[j, :, :RANK], wide[j + 1, :, :RANK]], 1)
            low = jnp.concatenate([wide[j, :, RANK:], wide[j + 1, :, RANK:]], 1)
            parts.append(jnp.concatenate([top, low], 0).astype(jnp.bfloat16))
        given = jnp.concatenate(parts, 1)
        both = dot(given, folded_ref[0]) + dot(given, folded_ref[1])
        own_ref[...] = both[:, :RANK]
        cross_ref[...] = both[:, RANK:]

    @pl.when(spot >= FOLDED)
    def _():
        copies = levels_copies(up_hbm, coup_hbm, up_ref, coup_ref, mats)
        for copy in copies:
            copy.start()
        for copy in copies:
            copy.wait()
        climb(wide, up_ref, coup_ref, own_ref, cross_ref, levels)


def climb(wide, up_ref, coup_ref, own_ref, cross_ref, levels):
    spot, half, place = position()
    for j, (line, z) in enumerate(MEMBERS):
        levels[0][0, line * LINE + z] = wide[j, :, :RANK]
        levels[0][1, line * LINE + z] = wide[j, :, RANK:]
    for h in range(1, TOPL + 1):
        count = PAIR >> h
        before = levels[h - 1][...].reshape(2, count, 2, 8, RANK)
        pairs = jnp.concatenate([before[:, :, 0], before[:, :, 1]], -1)
        mat = up_ref[h - 1].reshape(2 * RANK, RANK)
        levels[h][...] = dot_split(pairs.reshape(NRHS * count, 2 * RANK), mat).reshape(2, count, 8, RANK)

    fields = []
    for h in range(TOPL + 1):
        sides = [
            levels[h][:, q].reshape(NRHS, RANK) * used.astype(jnp.float32)
            for _, _, q, used in neighbours(h, spot, half, place)
        ]
        rows = jnp.concatenate([jnp.concatenate(sides[:2], 1), jnp.concatenate(sides[2:], 1)], 0)
        fields.append(dot_split(rows, coup_ref[h].reshape(2 * RANK, RANK)))
    incoming = fields[TOPL]
    for h in range(TOPL, 0, -1):
        parity = (spot >> (h - 1)) & 1
        incoming = fields[h - 1] + dot_split(incoming, up_ref[h - 1, parity], NT)
    own_ref[...] = incoming[:NRHS]
    cross_ref[...] = incoming[NRHS:]


def out_kernel(own_ref, cross_ref, field_ref, near_ref, transfer_ref, basis_ref, out_ref):
    incoming = own_ref[...] + cross_ref[...]
    spread = dot_split(incoming, transfer_ref[...].reshape(LEAF_DEV * RANK, RANK), NT)
    potential = (field_ref[...] + spread).astype(jnp.bfloat16)
    for t in range(LEAF_DEV):
        far = dot(potential[:, t * RANK : (t + 1) * RANK], basis_ref[t])
        at = slice(t * LEAF, (t + 1) * LEAF)
        out_ref[:, at] = (far + near_ref[:, at]).astype(jnp.bfloat16)


def crossed(values, count):
    route = []
    for line in range(1, count // LINE - 1, 2):
        for z in range(LINE):
            low = line * LINE + z
            route += [(low, low + LINE), (low + LINE, low)]
    return lax.ppermute(values, AXES, route)


def traded(values, count, odd):
    route = []
    for low in range(odd, count - 1, 2):
        route += [(low, low + 1), (low + 1, low)]
    return lax.ppermute(values, AXES, route)


def call(kernel, outs, scratch=(), ins=(), flops=0, moved=0, name=None, aliases=None):
    return pl.pallas_call(
        kernel,
        out_shape=[jax.ShapeDtypeStruct(shape, dtype) for shape, dtype in outs],
        in_specs=list(ins),
        out_specs=[VMEM] * len(outs),
        scratch_shapes=list(scratch),
        cost_estimate=pl.CostEstimate(flops=flops, bytes_accessed=moved, transcendentals=0),
        compiler_params=pltpu.CompilerParams(vmem_limit_bytes=24 * 2**20),
        input_output_aliases=aliases or {},
        name=name,
    )


def local(
    rhs,
    leaf_basis,
    leaf_transfer,
    leaf_coupling,
    coupling_sources,
    near_tiles,
    near_sources,
    top_transfer,
    cluster_coupling,
):
    bf16, f32 = jnp.bfloat16, jnp.float32
    count = lax.axis_size(AXES)
    width = LEAF_DEV * LEAF
    ranks = LEAF_DEV * RANK
    inputs = (
        rhs, leaf_basis, leaf_transfer, near_sources, coupling_sources,
        leaf_coupling, near_tiles, top_transfer, cluster_coupling,
    )
    inputs = [pltpu.with_memory_space_constraint(x, pltpu.HBM) for x in inputs]
    coeffs, sends, first, second, folded, *kept = call(
        coeff_kernel,
        [
            ((NRHS, ranks), bf16),
            ((PAIR * 8, 2 * RANK), bf16),
            ((NRHS, EDGE), bf16),
            ((NRHS, EDGE), bf16),
            ((2, PAIR * RANK, 2 * RANK), bf16),
        ]
        + [(x.shape, x.dtype) for x in inputs[:-2]],
        scratch=[pltpu.SemaphoreType.DMA((n,)) for n in (STAGED, HELD, 2)]
        + [pltpu.VMEM(x.shape, bf16) for x in inputs[-2:]]
        + [pltpu.VMEM((PAIR >> h, RANK, 2 * RANK), f32) for h in range(TOPL + 1)],
        ins=[HBM] * len(inputs),
        flops=2 * NRHS * ranks * (LEAF + RANK),
        moved=2**21,
        name="coeffs",
    )(*inputs)
    rhs, leaf_basis, leaf_transfer, near_sources, coupling_sources = kept[:STAGED]
    coupling_kept, tiles_kept = kept[STAGED:]
    pairs = [
        [(2 * k + line) * LINE + z for line, z in MEMBERS]
        for k in range(lax.axis_size("gy") // 2)
    ]
    got = lax.all_to_all(sends, ("gy", "gz"), 0, 0, tiled=True, axis_index_groups=pairs)
    first = traded(first, count, 1)
    second = traded(second, count, 0)
    near, field, _, _ = call(
        near_kernel,
        [((NRHS, width), f32), ((NRHS, ranks), f32)]
        + [(x.shape, x.dtype) for x in (coupling_kept, tiles_kept)],
        scratch=[
            pltpu.VMEM((LEAF_DEV + 2 * REACH + 1, NRHS, LEAF), bf16),
            pltpu.VMEM((LEAF_DEV + 2 * REACH + 1, NRHS, RANK), bf16),
            pltpu.SemaphoreType.DMA((HELD,)),
        ],
        ins=[SMEM, SMEM] + [VMEM] * 4 + [HBM] * 2 + [VMEM] * 2,
        aliases={8: 2, 9: 3},
        flops=2 * NRHS * LEAF_DEV * (NEAR * LEAF * LEAF + ADM * RANK * RANK),
        moved=2**21,
        name="near",
    )(near_sources, coupling_sources, rhs, coeffs, first, second, *inputs[STAGED:-2], coupling_kept, tiles_kept)
    own, cross = call(
        tree_kernel,
        [((NRHS, RANK), f32)] * 2,
        scratch=[pltpu.VMEM(x.shape, bf16) for x in inputs[-2:]]
        + [pltpu.SemaphoreType.DMA((2,))]
        + [pltpu.VMEM((2, PAIR >> h, 8, RANK), f32) for h in range(TOPL + 1)],
        ins=[VMEM] * 2 + [HBM] * 2,
        flops=2**23,
        moved=2**18,
        name="tree",
    )(got, folded, *inputs[-2:])
    cross = crossed(cross, count)
    return call(
        out_kernel,
        [((NRHS, width), bf16)],
        ins=[VMEM] * 6,
        flops=2 * NRHS * ranks * (LEAF + RANK),
        moved=2**18,
        name="out",
    )(own, cross, field, near, leaf_transfer, leaf_basis)[0]


def solution(mesh):
    placed = (
        P(None, AXES),
        P(AXES, None, None),
        P(AXES, None, None),
        P(AXES, None, None, None),
        P(AXES, None),
        P(AXES, None, None, None),
        P(AXES, None),
        P(),
        P(),
    )
    return jax.shard_map(
        local, mesh=mesh, in_specs=placed, out_specs=P(None, AXES), check_vma=False
    )
```

```python
import jax
import jax.numpy as jnp
from jax import lax
from jax.experimental import pallas as pl
from jax.experimental.pallas import tpu as pltpu
from jax.sharding import PartitionSpec as P

LEAF = 256
RANK = 64
NRHS = 16
NEAR = 3
ADM = 6
TOPL = 4
LEAF_DEV = 4
REACH = 2
LINE = 16
PAIR = 2 * LINE
LEADER = 11
MEMBERS = [(1, LEADER)] + [(line, z) for line in (0, 1) for z in [12, 11, 10, 9, 8, 7, 6, 5, 4, 3, 2, 1, 0, 15, 14, 13] if (line, z) != (1, LEADER)]
AXES = ("gx", "gy", "gz")
EDGE = REACH * (LEAF + RANK)
VMEM = pl.BlockSpec(memory_space=pltpu.VMEM)
SMEM = pl.BlockSpec(memory_space=pltpu.SMEM)
HBM = pl.BlockSpec(memory_space=pltpu.HBM)
STAGED = 5
HELD = 2
EARLY = 6
FOLDED = 4
NT = (((1,), (1,)), ((), ()))
NN = (((1,), (0,)), ((), ()))
TN = (((0,), (0,)), ((), ()))


def dot(a, b, dims=NN):
    return lax.dot_general(a, b, dims, preferred_element_type=jnp.float32)


def dot_split(a, b, dims=NN):
    high = a.astype(jnp.bfloat16)
    low = (a - high.astype(jnp.float32)).astype(jnp.bfloat16)
    both = dot(jnp.concatenate([high, low], 0), b, dims)
    return both[: a.shape[0]] + both[a.shape[0] :]


def dot_wide(a, b, dims=NN):
    high = b.astype(jnp.bfloat16)
    low = (b - high.astype(jnp.float32)).astype(jnp.bfloat16)
    both = dot(a, jnp.concatenate([high, low], 1), dims)
    return both[:, : b.shape[1]] + both[:, b.shape[1] :]


def position():
    spot = lax.axis_index("gz")
    half = lax.axis_index("gy") & 1
    return spot, half, half * LINE + spot


def neighbours(h, spot, half, place):
    count = PAIR >> h
    q, low = place >> h, spot >> h
    return [
        (0, 0, jnp.maximum(q - 1, 0), q > 0),
        (0, 1, jnp.minimum(q + 1, count - 1), q < count - 1),
        (1, 0, count - 1, (half == 1) & (low == 0)),
        (1, 1, 0, (half == 0) & (low == (LINE >> h) - 1)),
    ]


def fold(up_ref, coup_ref, folded_ref, maps):
    spot, half, place = position()
    maps[TOPL][...] = jnp.zeros_like(maps[TOPL])
    down = [None]
    for h in range(1, TOPL + 1):
        step = up_ref[h - 1, (spot >> (h - 1)) & 1]
        down.append(step.T.astype(jnp.float32) if h == 1 else dot_wide(step, down[-1], TN))
    zero = jnp.zeros((RANK, RANK), jnp.float32)
    for h in range(TOPL, -1, -1):
        for to, side, q, used in neighbours(h, spot, half, place):
            mat = coup_ref[h, side]
            term = dot_wide(mat, down[h]) if h else mat.astype(jnp.float32)
            term = term * used.astype(jnp.float32)
            maps[h][q] += jnp.concatenate([zero, term] if to else [term, zero], 1)
        if h:
            mat = up_ref[h - 1].reshape(2 * RANK, RANK)
            for q in range(PAIR >> h):
                maps[h - 1][2 * q : 2 * q + 2] = dot_wide(mat, maps[h][q]).reshape(2, RANK, 2 * RANK)
    for j, (line, z) in enumerate(MEMBERS):
        values = maps[0][line * LINE + z]
        high = values.astype(jnp.bfloat16)
        at = slice(j * RANK, (j + 1) * RANK)
        folded_ref[0, at, :] = high
        folded_ref[1, at, :] = (values - high.astype(jnp.float32)).astype(jnp.bfloat16)


def hold(staged, kept, done):
    return [pltpu.make_async_copy(staged[i], kept[i], done.at[i]) for i in range(HELD)]


def levels_copies(up_hbm, coup_hbm, up_ref, coup_ref, done):
    return [
        pltpu.make_async_copy(up_hbm, up_ref, done.at[0]),
        pltpu.make_async_copy(coup_hbm, coup_ref, done.at[1]),
    ]


def coeff_kernel(*refs):
    count = STAGED + HELD
    staged, (up_hbm, coup_hbm), refs = refs[:count], refs[count : count + 2], refs[count + 2 :]
    coeffs_ref, sends_hbm, first_ref, second_ref, folded_ref = refs[:5]
    kept, (done, held, mats), refs = refs[5 : count + 5], refs[count + 5 : count + 8], refs[count + 8 :]
    up_ref, coup_ref, sends_ref, sent, maps = *refs[:4], refs[4:]
    spot = lax.axis_index("gz")
    early, folding = spot < EARLY, spot < FOLDED
    copies = [
        pltpu.make_async_copy(staged[i], kept[i], done.at[i]) for i in range(STAGED)
    ]
    for copy in copies:
        copy.start()

    @pl.when(early)
    def _():
        for copy in hold(staged[STAGED:], kept[STAGED:], held):
            copy.start()

    @pl.when(folding)
    def _():
        for copy in levels_copies(up_hbm, coup_hbm, up_ref, coup_ref, mats):
            copy.start()

    rhs_ref, basis_ref, transfer_ref = kept[:3]
    copies[0].wait()
    copies[1].wait()
    parts = []
    for t in range(LEAF_DEV):
        block = rhs_ref[:, t * LEAF : (t + 1) * LEAF]
        parts.append(dot(block, basis_ref[t], NT).astype(jnp.bfloat16))
    copies[2].wait()
    coeffs = jnp.concatenate(parts, 1)
    root = dot(coeffs, transfer_ref[...].reshape(LEAF_DEV * RANK, RANK))
    packed = jnp.concatenate([root[:8], root[8:]], 1)
    packed = jnp.concatenate([packed, packed], 0).astype(jnp.bfloat16)
    for j in range(PAIR // 2):
        sends_ref[16 * j : 16 * (j + 1), :] = packed
    sending = pltpu.make_async_copy(sends_ref, sends_hbm, sent.at[0])
    sending.start()
    coeffs_ref[...] = coeffs
    wide = REACH * LEAF
    tail = jnp.concatenate([rhs_ref[:, (LEAF_DEV - REACH) * LEAF :], coeffs[:, (LEAF_DEV - REACH) * RANK :]], 1)
    head = jnp.concatenate([rhs_ref[:, :wide], coeffs[:, : REACH * RANK]], 1)
    odd = jnp.broadcast_to(spot & 1, tail.shape) == 1
    first_ref[...] = jnp.where(odd, tail, head)
    second_ref[...] = jnp.where(odd, head, tail)
    for copy in copies[3:]:
        copy.wait()
    sending.wait()

    @pl.when(folding)
    def _():
        for copy in levels_copies(up_hbm, coup_hbm, up_ref, coup_ref, mats):
            copy.wait()
        fold(up_ref, coup_ref, folded_ref, maps)

    @pl.when(early)
    def _():
        for copy in hold(staged[STAGED:], kept[STAGED:], held):
            copy.wait()


def near_kernel(
    near_src, coup_src, rhs_ref, coeffs_ref, first_ref, second_ref, coupling_hbm, tiles_hbm,
    coupling_in, tiles_in, near_ref, field_ref, coupling_ref, tiles_ref, blocks, leaf_coeffs, held,
):
    late = lax.axis_index("gz") >= EARLY

    @pl.when(late)
    def _():
        for copy in hold([coupling_hbm, tiles_hbm], [coupling_ref, tiles_ref], held):
            copy.start()

    own = near_src[0, 0]
    anchor = own - REACH
    none = LEAF_DEV + 2 * REACH
    wide = REACH * LEAF
    above = REACH + LEAF_DEV
    odd = lax.axis_index("gz") & 1
    for side_ref, start in ((first_ref, above * odd), (second_ref, above * (1 - odd))):
        for i in range(REACH):
            blocks[start + i] = side_ref[:, i * LEAF : (i + 1) * LEAF]
            leaf_coeffs[start + i] = side_ref[:, wide + i * RANK : wide + (i + 1) * RANK]
    for t in range(LEAF_DEV):
        blocks[REACH + t] = rhs_ref[:, t * LEAF : (t + 1) * LEAF]
        leaf_coeffs[REACH + t] = coeffs_ref[:, t * RANK : (t + 1) * RANK]
    blocks[none] = jnp.zeros((NRHS, LEAF), jnp.bfloat16)
    leaf_coeffs[none] = jnp.zeros((NRHS, RANK), jnp.bfloat16)

    def place(source):
        return jnp.where(source >= 0, jnp.clip(source - anchor, 0, none - 1), none)

    @pl.when(late)
    def _():
        for copy in hold([coupling_hbm, tiles_hbm], [coupling_ref, tiles_ref], held):
            copy.wait()

    fields = []
    for t in range(LEAF_DEV):
        picked = jnp.concatenate([blocks[place(near_src[t, n])] for n in range(NEAR)], 1)
        near_ref[:, t * LEAF : (t + 1) * LEAF] = dot(picked, tiles_ref[t].reshape(NEAR * LEAF, LEAF))
        taken = jnp.concatenate([leaf_coeffs[place(coup_src[t, a])] for a in range(ADM)], 1)
        fields.append(dot(taken, coupling_ref[t].reshape(ADM * RANK, RANK)))
    field_ref[...] = jnp.concatenate(fields, 1)


def tree_kernel(got_ref, folded_ref, up_hbm, coup_hbm, own_ref, cross_ref, up_ref, coup_ref, mats, *levels):
    spot, half, place = position()
    wide = got_ref[...].astype(jnp.float32).reshape(PAIR, 8, 2 * RANK)

    @pl.when(spot < FOLDED)
    def _():
        parts = []
        for j in range(0, PAIR, 2):
            top = jnp.concatenate([wide[j, :, :RANK], wide[j + 1, :, :RANK]], 1)
            low = jnp.concatenate([wide[j, :, RANK:], wide[j + 1, :, RANK:]], 1)
            parts.append(jnp.concatenate([top, low], 0).astype(jnp.bfloat16))
        given = jnp.concatenate(parts, 1)
        both = dot(given, folded_ref[0]) + dot(given, folded_ref[1])
        own_ref[...] = both[:, :RANK]
        cross_ref[...] = both[:, RANK:]

    @pl.when(spot >= FOLDED)
    def _():
        copies = levels_copies(up_hbm, coup_hbm, up_ref, coup_ref, mats)
        for copy in copies:
            copy.start()
        for copy in copies:
            copy.wait()
        climb(wide, up_ref, coup_ref, own_ref, cross_ref, levels)


def climb(wide, up_ref, coup_ref, own_ref, cross_ref, levels):
    spot, half, place = position()
    for j, (line, z) in enumerate(MEMBERS):
        levels[0][0, line * LINE + z] = wide[j, :, :RANK]
        levels[0][1, line * LINE + z] = wide[j, :, RANK:]
    for h in range(1, TOPL + 1):
        count = PAIR >> h
        before = levels[h - 1][...].reshape(2, count, 2, 8, RANK)
        pairs = jnp.concatenate([before[:, :, 0], before[:, :, 1]], -1)
        mat = up_ref[h - 1].reshape(2 * RANK, RANK)
        levels[h][...] = dot_split(pairs.reshape(NRHS * count, 2 * RANK), mat).reshape(2, count, 8, RANK)

    fields = []
    for h in range(TOPL + 1):
        sides = [
            levels[h][:, q].reshape(NRHS, RANK) * used.astype(jnp.float32)
            for _, _, q, used in neighbours(h, spot, half, place)
        ]
        rows = jnp.concatenate([jnp.concatenate(sides[:2], 1), jnp.concatenate(sides[2:], 1)], 0)
        fields.append(dot_split(rows, coup_ref[h].reshape(2 * RANK, RANK)))
    incoming = fields[TOPL]
    for h in range(TOPL, 0, -1):
        parity = (spot >> (h - 1)) & 1
        incoming = fields[h - 1] + dot_split(incoming, up_ref[h - 1, parity], NT)
    own_ref[...] = incoming[:NRHS]
    cross_ref[...] = incoming[NRHS:]


def out_kernel(own_ref, cross_ref, field_ref, near_ref, transfer_ref, basis_ref, out_ref):
    incoming = own_ref[...] + cross_ref[...]
    spread = dot_split(incoming, transfer_ref[...].reshape(LEAF_DEV * RANK, RANK), NT)
    potential = (field_ref[...] + spread).astype(jnp.bfloat16)
    for t in range(LEAF_DEV):
        far = dot(potential[:, t * RANK : (t + 1) * RANK], basis_ref[t])
        at = slice(t * LEAF, (t + 1) * LEAF)
        out_ref[:, at] = (far + near_ref[:, at]).astype(jnp.bfloat16)


def crossed(values, count):
    route = []
    for line in range(1, count // LINE - 1, 2):
        for z in range(LINE):
            low = line * LINE + z
            route += [(low, low + LINE), (low + LINE, low)]
    return lax.ppermute(values, AXES, route)


def traded(values, count, odd):
    route = []
    for low in range(odd, count - 1, 2):
        route += [(low, low + 1), (low + 1, low)]
    return lax.ppermute(values, AXES, route)


def call(kernel, outs, scratch=(), ins=(), flops=0, moved=0, name=None, aliases=None, hbm=()):
    return pl.pallas_call(
        kernel,
        out_shape=[jax.ShapeDtypeStruct(shape, dtype) for shape, dtype in outs],
        in_specs=list(ins),
        out_specs=[HBM if i in hbm else VMEM for i in range(len(outs))],
        scratch_shapes=list(scratch),
        cost_estimate=pl.CostEstimate(flops=flops, bytes_accessed=moved, transcendentals=0),
        compiler_params=pltpu.CompilerParams(vmem_limit_bytes=24 * 2**20),
        input_output_aliases=aliases or {},
        name=name,
    )


def local(
    rhs,
    leaf_basis,
    leaf_transfer,
    leaf_coupling,
    coupling_sources,
    near_tiles,
    near_sources,
    top_transfer,
    cluster_coupling,
):
    bf16, f32 = jnp.bfloat16, jnp.float32
    count = lax.axis_size(AXES)
    width = LEAF_DEV * LEAF
    ranks = LEAF_DEV * RANK
    inputs = (
        rhs, leaf_basis, leaf_transfer, near_sources, coupling_sources,
        leaf_coupling, near_tiles, top_transfer, cluster_coupling,
    )
    inputs = [pltpu.with_memory_space_constraint(x, pltpu.HBM) for x in inputs]
    coeffs, sends, first, second, folded, *kept = call(
        coeff_kernel,
        [
            ((NRHS, ranks), bf16),
            ((PAIR * 8, 2 * RANK), bf16),
            ((NRHS, EDGE), bf16),
            ((NRHS, EDGE), bf16),
            ((2, PAIR * RANK, 2 * RANK), bf16),
        ]
        + [(x.shape, x.dtype) for x in inputs[:-2]],
        scratch=[pltpu.SemaphoreType.DMA((n,)) for n in (STAGED, HELD, 2)]
        + [pltpu.VMEM(x.shape, bf16) for x in inputs[-2:]]
        + [pltpu.VMEM((PAIR * 8, 2 * RANK), bf16), pltpu.SemaphoreType.DMA((1,))]
        + [pltpu.VMEM((PAIR >> h, RANK, 2 * RANK), f32) for h in range(TOPL + 1)],
        ins=[HBM] * len(inputs),
        hbm=[1],
        flops=2 * NRHS * ranks * (LEAF + RANK),
        moved=2**21,
        name="coeffs",
    )(*inputs)
    rhs, leaf_basis, leaf_transfer, near_sources, coupling_sources = kept[:STAGED]
    coupling_kept, tiles_kept = kept[STAGED:]
    pairs = [
        [(2 * k + line) * LINE + z for line, z in MEMBERS]
        for k in range(lax.axis_size("gy") // 2)
    ]
    got = lax.all_to_all(sends, ("gy", "gz"), 0, 0, tiled=True, axis_index_groups=pairs)
    first = traded(first, count, 1)
    second = traded(second, count, 0)
    near, field, _, _ = call(
        near_kernel,
        [((NRHS, width), f32), ((NRHS, ranks), f32)]
        + [(x.shape, x.dtype) for x in (coupling_kept, tiles_kept)],
        scratch=[
            pltpu.VMEM((LEAF_DEV + 2 * REACH + 1, NRHS, LEAF), bf16),
            pltpu.VMEM((LEAF_DEV + 2 * REACH + 1, NRHS, RANK), bf16),
            pltpu.SemaphoreType.DMA((HELD,)),
        ],
        ins=[SMEM, SMEM] + [VMEM] * 4 + [HBM] * 2 + [VMEM] * 2,
        aliases={8: 2, 9: 3},
        flops=2 * NRHS * LEAF_DEV * (NEAR * LEAF * LEAF + ADM * RANK * RANK),
        moved=2**21,
        name="near",
    )(near_sources, coupling_sources, rhs, coeffs, first, second, *inputs[STAGED:-2], coupling_kept, tiles_kept)
    own, cross = call(
        tree_kernel,
        [((NRHS, RANK), f32)] * 2,
        scratch=[pltpu.VMEM(x.shape, bf16) for x in inputs[-2:]]
        + [pltpu.SemaphoreType.DMA((2,))]
        + [pltpu.VMEM((2, PAIR >> h, 8, RANK), f32) for h in range(TOPL + 1)],
        ins=[VMEM] * 2 + [HBM] * 2,
        flops=2**23,
        moved=2**18,
        name="tree",
    )(got, folded, *inputs[-2:])
    cross = crossed(cross, count)
    return call(
        out_kernel,
        [((NRHS, width), bf16)],
        ins=[VMEM] * 6,
        flops=2 * NRHS * ranks * (LEAF + RANK),
        moved=2**18,
        name="out",
    )(own, cross, field, near, leaf_transfer, leaf_basis)[0]


def solution(mesh):
    placed = (
        P(None, AXES),
        P(AXES, None, None),
        P(AXES, None, None),
        P(AXES, None, None, None),
        P(AXES, None),
        P(AXES, None, None, None),
        P(AXES, None),
        P(),
        P(),
    )
    return jax.shard_map(
        local, mesh=mesh, in_specs=placed, out_specs=P(None, AXES), check_vma=False
    )
```

```python
import jax
import jax.numpy as jnp
from jax import lax
from jax.experimental import pallas as pl
from jax.experimental.pallas import tpu as pltpu
from jax.sharding import PartitionSpec as P

LEAF = 256
RANK = 64
NRHS = 16
NEAR = 3
ADM = 6
TOPL = 4
LEAF_DEV = 4
REACH = 2
LINE = 16
PAIR = 2 * LINE
LEADER = 11
MEMBERS = [(1, LEADER)] + [(line, z) for line in (0, 1) for z in [12, 11, 10, 9, 8, 7, 6, 5, 4, 3, 2, 1, 0, 15, 14, 13] if (line, z) != (1, LEADER)]
AXES = ("gx", "gy", "gz")
EDGE = REACH * (LEAF + RANK)
VMEM = pl.BlockSpec(memory_space=pltpu.VMEM)
SMEM = pl.BlockSpec(memory_space=pltpu.SMEM)
HBM = pl.BlockSpec(memory_space=pltpu.HBM)
STAGED = 5
HELD = 2
EARLY = 6
FOLDED = 4
NT = (((1,), (1,)), ((), ()))
NN = (((1,), (0,)), ((), ()))
TN = (((0,), (0,)), ((), ()))


def dot(a, b, dims=NN):
    return lax.dot_general(a, b, dims, preferred_element_type=jnp.float32)


def dot_split(a, b, dims=NN):
    high = a.astype(jnp.bfloat16)
    low = (a - high.astype(jnp.float32)).astype(jnp.bfloat16)
    both = dot(jnp.concatenate([high, low], 0), b, dims)
    return both[: a.shape[0]] + both[a.shape[0] :]


def dot_wide(a, b, dims=NN):
    high = b.astype(jnp.bfloat16)
    low = (b - high.astype(jnp.float32)).astype(jnp.bfloat16)
    both = dot(a, jnp.concatenate([high, low], 1), dims)
    return both[:, : b.shape[1]] + both[:, b.shape[1] :]


def position():
    spot = lax.axis_index("gz")
    half = lax.axis_index("gy") & 1
    return spot, half, half * LINE + spot


def neighbours(h, spot, half, place):
    count = PAIR >> h
    q, low = place >> h, spot >> h
    return [
        (0, 0, jnp.maximum(q - 1, 0), q > 0),
        (0, 1, jnp.minimum(q + 1, count - 1), q < count - 1),
        (1, 0, count - 1, (half == 1) & (low == 0)),
        (1, 1, 0, (half == 0) & (low == (LINE >> h) - 1)),
    ]


def fold(up_ref, coup_ref, folded_ref, maps):
    spot, half, place = position()
    maps[TOPL][...] = jnp.zeros_like(maps[TOPL])
    down = [None]
    for h in range(1, TOPL + 1):
        step = up_ref[h - 1, (spot >> (h - 1)) & 1]
        down.append(step.T.astype(jnp.float32) if h == 1 else dot_wide(step, down[-1], TN))
    zero = jnp.zeros((RANK, RANK), jnp.float32)
    for h in range(TOPL, -1, -1):
        for to, side, q, used in neighbours(h, spot, half, place):
            mat = coup_ref[h, side]
            term = dot_wide(mat, down[h]) if h else mat.astype(jnp.float32)
            term = term * used.astype(jnp.float32)
            maps[h][q] += jnp.concatenate([zero, term] if to else [term, zero], 1)
        if h:
            mat = up_ref[h - 1].reshape(2 * RANK, RANK)
            for q in range(PAIR >> h):
                maps[h - 1][2 * q : 2 * q + 2] = dot_wide(mat, maps[h][q]).reshape(2, RANK, 2 * RANK)
    for j, (line, z) in enumerate(MEMBERS):
        values = maps[0][line * LINE + z]
        high = values.astype(jnp.bfloat16)
        at = slice(j * RANK, (j + 1) * RANK)
        folded_ref[0, at, :] = high
        folded_ref[1, at, :] = (values - high.astype(jnp.float32)).astype(jnp.bfloat16)


def hold(staged, kept, done):
    return [pltpu.make_async_copy(staged[i], kept[i], done.at[i]) for i in range(HELD)]


def levels_copies(up_hbm, coup_hbm, up_ref, coup_ref, done):
    return [
        pltpu.make_async_copy(up_hbm, up_ref, done.at[0]),
        pltpu.make_async_copy(coup_hbm, coup_ref, done.at[1]),
    ]


def coeff_kernel(*refs):
    count = STAGED + HELD
    staged, (up_hbm, coup_hbm), refs = refs[:count], refs[count : count + 2], refs[count + 2 :]
    coeffs_ref, sends_hbm, first_ref, second_ref, folded_ref = refs[:5]
    kept, (done, held, mats), refs = refs[5 : count + 5], refs[count + 5 : count + 8], refs[count + 8 :]
    up_ref, coup_ref, sends_ref, sent, maps = *refs[:4], refs[4:]
    spot = lax.axis_index("gz")
    early, folding = spot < EARLY, spot < FOLDED
    copies = [
        pltpu.make_async_copy(staged[i], kept[i], done.at[i]) for i in range(STAGED)
    ]
    for i in (1, 0, 2):
        copies[i].start()

    @pl.when(early)
    def _():
        for copy in hold(staged[STAGED:], kept[STAGED:], held):
            copy.start()

    @pl.when(folding)
    def _():
        for copy in levels_copies(up_hbm, coup_hbm, up_ref, coup_ref, mats):
            copy.start()

    rhs_ref, basis_ref, transfer_ref = kept[:3]
    copies[1].wait()
    copies[0].wait()
    parts = []
    for t in range(LEAF_DEV):
        block = rhs_ref[:, t * LEAF : (t + 1) * LEAF]
        parts.append(dot(block, basis_ref[t], NT).astype(jnp.bfloat16))
    for copy in copies[3:]:
        copy.start()
    copies[2].wait()
    coeffs = jnp.concatenate(parts, 1)
    root = dot(coeffs, transfer_ref[...].reshape(LEAF_DEV * RANK, RANK))
    packed = jnp.concatenate([root[:8], root[8:]], 1)
    packed = jnp.concatenate([packed, packed], 0).astype(jnp.bfloat16)
    for j in range(PAIR // 2):
        sends_ref[16 * j : 16 * (j + 1), :] = packed
    sending = pltpu.make_async_copy(sends_ref, sends_hbm, sent.at[0])
    sending.start()
    coeffs_ref[...] = coeffs
    wide = REACH * LEAF
    tail = jnp.concatenate([rhs_ref[:, (LEAF_DEV - REACH) * LEAF :], coeffs[:, (LEAF_DEV - REACH) * RANK :]], 1)
    head = jnp.concatenate([rhs_ref[:, :wide], coeffs[:, : REACH * RANK]], 1)
    odd = jnp.broadcast_to(spot & 1, tail.shape) == 1
    first_ref[...] = jnp.where(odd, tail, head)
    second_ref[...] = jnp.where(odd, head, tail)
    for copy in copies[3:]:
        copy.wait()
    sending.wait()

    @pl.when(folding)
    def _():
        for copy in levels_copies(up_hbm, coup_hbm, up_ref, coup_ref, mats):
            copy.wait()
        fold(up_ref, coup_ref, folded_ref, maps)

    @pl.when(early)
    def _():
        for copy in hold(staged[STAGED:], kept[STAGED:], held):
            copy.wait()


def near_kernel(
    near_src, coup_src, rhs_ref, coeffs_ref, first_ref, second_ref, coupling_hbm, tiles_hbm,
    coupling_in, tiles_in, near_ref, field_ref, coupling_ref, tiles_ref, blocks, leaf_coeffs, held,
):
    late = lax.axis_index("gz") >= EARLY

    @pl.when(late)
    def _():
        for copy in hold([coupling_hbm, tiles_hbm], [coupling_ref, tiles_ref], held):
            copy.start()

    own = near_src[0, 0]
    anchor = own - REACH
    none = LEAF_DEV + 2 * REACH
    wide = REACH * LEAF
    above = REACH + LEAF_DEV
    odd = lax.axis_index("gz") & 1
    for side_ref, start in ((first_ref, above * odd), (second_ref, above * (1 - odd))):
        for i in range(REACH):
            blocks[start + i] = side_ref[:, i * LEAF : (i + 1) * LEAF]
            leaf_coeffs[start + i] = side_ref[:, wide + i * RANK : wide + (i + 1) * RANK]
    for t in range(LEAF_DEV):
        blocks[REACH + t] = rhs_ref[:, t * LEAF : (t + 1) * LEAF]
        leaf_coeffs[REACH + t] = coeffs_ref[:, t * RANK : (t + 1) * RANK]
    blocks[none] = jnp.zeros((NRHS, LEAF), jnp.bfloat16)
    leaf_coeffs[none] = jnp.zeros((NRHS, RANK), jnp.bfloat16)

    def place(source):
        return jnp.where(source >= 0, jnp.clip(source - anchor, 0, none - 1), none)

    @pl.when(late)
    def _():
        for copy in hold([coupling_hbm, tiles_hbm], [coupling_ref, tiles_ref], held):
            copy.wait()

    fields = []
    for t in range(LEAF_DEV):
        picked = jnp.concatenate([blocks[place(near_src[t, n])] for n in range(NEAR)], 1)
        near_ref[:, t * LEAF : (t + 1) * LEAF] = dot(picked, tiles_ref[t].reshape(NEAR * LEAF, LEAF))
        taken = jnp.concatenate([leaf_coeffs[place(coup_src[t, a])] for a in range(ADM)], 1)
        fields.append(dot(taken, coupling_ref[t].reshape(ADM * RANK, RANK)))
    field_ref[...] = jnp.concatenate(fields, 1)


def tree_kernel(got_ref, folded_ref, up_hbm, coup_hbm, own_ref, cross_ref, up_ref, coup_ref, mats, *levels):
    spot, half, place = position()
    wide = got_ref[...].astype(jnp.float32).reshape(PAIR, 8, 2 * RANK)

    @pl.when(spot < FOLDED)
    def _():
        parts = []
        for j in range(0, PAIR, 2):
            top = jnp.concatenate([wide[j, :, :RANK], wide[j + 1, :, :RANK]], 1)
            low = jnp.concatenate([wide[j, :, RANK:], wide[j + 1, :, RANK:]], 1)
            parts.append(jnp.concatenate([top, low], 0).astype(jnp.bfloat16))
        given = jnp.concatenate(parts, 1)
        both = dot(given, folded_ref[0]) + dot(given, folded_ref[1])
        own_ref[...] = both[:, :RANK]
        cross_ref[...] = both[:, RANK:]

    @pl.when(spot >= FOLDED)
    def _():
        copies = levels_copies(up_hbm, coup_hbm, up_ref, coup_ref, mats)
        for copy in copies:
            copy.start()
        for copy in copies:
            copy.wait()
        climb(wide, up_ref, coup_ref, own_ref, cross_ref, levels)


def climb(wide, up_ref, coup_ref, own_ref, cross_ref, levels):
    spot, half, place = position()
    for j, (line, z) in enumerate(MEMBERS):
        levels[0][0, line * LINE + z] = wide[j, :, :RANK]
        levels[0][1, line * LINE + z] = wide[j, :, RANK:]
    for h in range(1, TOPL + 1):
        count = PAIR >> h
        before = levels[h - 1][...].reshape(2, count, 2, 8, RANK)
        pairs = jnp.concatenate([before[:, :, 0], before[:, :, 1]], -1)
        mat = up_ref[h - 1].reshape(2 * RANK, RANK)
        levels[h][...] = dot_split(pairs.reshape(NRHS * count, 2 * RANK), mat).reshape(2, count, 8, RANK)

    fields = []
    for h in range(TOPL + 1):
        sides = [
            levels[h][:, q].reshape(NRHS, RANK) * used.astype(jnp.float32)
            for _, _, q, used in neighbours(h, spot, half, place)
        ]
        rows = jnp.concatenate([jnp.concatenate(sides[:2], 1), jnp.concatenate(sides[2:], 1)], 0)
        fields.append(dot_split(rows, coup_ref[h].reshape(2 * RANK, RANK)))
    incoming = fields[TOPL]
    for h in range(TOPL, 0, -1):
        parity = (spot >> (h - 1)) & 1
        incoming = fields[h - 1] + dot_split(incoming, up_ref[h - 1, parity], NT)
    own_ref[...] = incoming[:NRHS]
    cross_ref[...] = incoming[NRHS:]


def out_kernel(own_ref, cross_ref, field_ref, near_ref, transfer_ref, basis_ref, out_ref):
    incoming = own_ref[...] + cross_ref[...]
    spread = dot_split(incoming, transfer_ref[...].reshape(LEAF_DEV * RANK, RANK), NT)
    potential = (field_ref[...] + spread).astype(jnp.bfloat16)
    for t in range(LEAF_DEV):
        far = dot(potential[:, t * RANK : (t + 1) * RANK], basis_ref[t])
        at = slice(t * LEAF, (t + 1) * LEAF)
        out_ref[:, at] = (far + near_ref[:, at]).astype(jnp.bfloat16)


def crossed(values, count):
    route = []
    for line in range(1, count // LINE - 1, 2):
        for z in range(LINE):
            low = line * LINE + z
            route += [(low, low + LINE), (low + LINE, low)]
    return lax.ppermute(values, AXES, route)


def traded(values, count, odd):
    route = []
    for low in range(odd, count - 1, 2):
        route += [(low, low + 1), (low + 1, low)]
    return lax.ppermute(values, AXES, route)


def call(kernel, outs, scratch=(), ins=(), flops=0, moved=0, name=None, aliases=None, hbm=()):
    return pl.pallas_call(
        kernel,
        out_shape=[jax.ShapeDtypeStruct(shape, dtype) for shape, dtype in outs],
        in_specs=list(ins),
        out_specs=[HBM if i in hbm else VMEM for i in range(len(outs))],
        scratch_shapes=list(scratch),
        cost_estimate=pl.CostEstimate(flops=flops, bytes_accessed=moved, transcendentals=0),
        compiler_params=pltpu.CompilerParams(vmem_limit_bytes=24 * 2**20),
        input_output_aliases=aliases or {},
        name=name,
    )


def local(
    rhs,
    leaf_basis,
    leaf_transfer,
    leaf_coupling,
    coupling_sources,
    near_tiles,
    near_sources,
    top_transfer,
    cluster_coupling,
):
    bf16, f32 = jnp.bfloat16, jnp.float32
    count = lax.axis_size(AXES)
    width = LEAF_DEV * LEAF
    ranks = LEAF_DEV * RANK
    inputs = (
        rhs, leaf_basis, leaf_transfer, near_sources, coupling_sources,
        leaf_coupling, near_tiles, top_transfer, cluster_coupling,
    )
    inputs = [pltpu.with_memory_space_constraint(x, pltpu.HBM) for x in inputs]
    coeffs, sends, first, second, folded, *kept = call(
        coeff_kernel,
        [
            ((NRHS, ranks), bf16),
            ((PAIR * 8, 2 * RANK), bf16),
            ((NRHS, EDGE), bf16),
            ((NRHS, EDGE), bf16),
            ((2, PAIR * RANK, 2 * RANK), bf16),
        ]
        + [(x.shape, x.dtype) for x in inputs[:-2]],
        scratch=[pltpu.SemaphoreType.DMA((n,)) for n in (STAGED, HELD, 2)]
        + [pltpu.VMEM(x.shape, bf16) for x in inputs[-2:]]
        + [pltpu.VMEM((PAIR * 8, 2 * RANK), bf16), pltpu.SemaphoreType.DMA((1,))]
        + [pltpu.VMEM((PAIR >> h, RANK, 2 * RANK), f32) for h in range(TOPL + 1)],
        ins=[HBM] * len(inputs),
        hbm=[1],
        flops=2 * NRHS * ranks * (LEAF + RANK),
        moved=2**21,
        name="coeffs",
    )(*inputs)
    rhs, leaf_basis, leaf_transfer, near_sources, coupling_sources = kept[:STAGED]
    coupling_kept, tiles_kept = kept[STAGED:]
    pairs = [
        [(2 * k + line) * LINE + z for line, z in MEMBERS]
        for k in range(lax.axis_size("gy") // 2)
    ]
    got = lax.all_to_all(sends, ("gy", "gz"), 0, 0, tiled=True, axis_index_groups=pairs)
    first = traded(first, count, 1)
    second = traded(second, count, 0)
    near, field, _, _ = call(
        near_kernel,
        [((NRHS, width), f32), ((NRHS, ranks), f32)]
        + [(x.shape, x.dtype) for x in (coupling_kept, tiles_kept)],
        scratch=[
            pltpu.VMEM((LEAF_DEV + 2 * REACH + 1, NRHS, LEAF), bf16),
            pltpu.VMEM((LEAF_DEV + 2 * REACH + 1, NRHS, RANK), bf16),
            pltpu.SemaphoreType.DMA((HELD,)),
        ],
        ins=[SMEM, SMEM] + [VMEM] * 4 + [HBM] * 2 + [VMEM] * 2,
        aliases={8: 2, 9: 3},
        flops=2 * NRHS * LEAF_DEV * (NEAR * LEAF * LEAF + ADM * RANK * RANK),
        moved=2**21,
        name="near",
    )(near_sources, coupling_sources, rhs, coeffs, first, second, *inputs[STAGED:-2], coupling_kept, tiles_kept)
    own, cross = call(
        tree_kernel,
        [((NRHS, RANK), f32)] * 2,
        scratch=[pltpu.VMEM(x.shape, bf16) for x in inputs[-2:]]
        + [pltpu.SemaphoreType.DMA((2,))]
        + [pltpu.VMEM((2, PAIR >> h, 8, RANK), f32) for h in range(TOPL + 1)],
        ins=[VMEM] * 2 + [HBM] * 2,
        flops=2**23,
        moved=2**18,
        name="tree",
    )(got, folded, *inputs[-2:])
    cross = crossed(cross, count)
    return call(
        out_kernel,
        [((NRHS, width), bf16)],
        ins=[VMEM] * 6,
        flops=2 * NRHS * ranks * (LEAF + RANK),
        moved=2**18,
        name="out",
    )(own, cross, field, near, leaf_transfer, leaf_basis)[0]


def solution(mesh):
    placed = (
        P(None, AXES),
        P(AXES, None, None),
        P(AXES, None, None),
        P(AXES, None, None, None),
        P(AXES, None),
        P(AXES, None, None, None),
        P(AXES, None),
        P(),
        P(),
    )
    return jax.shard_map(
        local, mesh=mesh, in_specs=placed, out_specs=P(None, AXES), check_vma=False
    )
```

```python
import jax
import jax.numpy as jnp
from jax import lax
from jax.experimental import pallas as pl
from jax.experimental.pallas import tpu as pltpu
from jax.sharding import PartitionSpec as P

LEAF = 256
RANK = 64
NRHS = 16
NEAR = 3
ADM = 6
TOPL = 4
LEAF_DEV = 4
REACH = 2
LINE = 16
PAIR = 2 * LINE
LEADER = 11
MEMBERS = [(1, LEADER)] + [(line, z) for line in (0, 1) for z in [12, 11, 10, 9, 8, 7, 6, 5, 4, 3, 2, 1, 0, 15, 14, 13] if (line, z) != (1, LEADER)]
AXES = ("gx", "gy", "gz")
EDGE = REACH * (LEAF + RANK)
VMEM = pl.BlockSpec(memory_space=pltpu.VMEM)
SMEM = pl.BlockSpec(memory_space=pltpu.SMEM)
HBM = pl.BlockSpec(memory_space=pltpu.HBM)
STAGED = 5
HELD = 2
EARLY = 6
FOLDED = 4
NT = (((1,), (1,)), ((), ()))
NN = (((1,), (0,)), ((), ()))
TN = (((0,), (0,)), ((), ()))


def dot(a, b, dims=NN):
    return lax.dot_general(a, b, dims, preferred_element_type=jnp.float32)


def dot_split(a, b, dims=NN):
    high = a.astype(jnp.bfloat16)
    low = (a - high.astype(jnp.float32)).astype(jnp.bfloat16)
    both = dot(jnp.concatenate([high, low], 0), b, dims)
    return both[: a.shape[0]] + both[a.shape[0] :]


def dot_wide(a, b, dims=NN):
    high = b.astype(jnp.bfloat16)
    low = (b - high.astype(jnp.float32)).astype(jnp.bfloat16)
    both = dot(a, jnp.concatenate([high, low], 1), dims)
    return both[:, : b.shape[1]] + both[:, b.shape[1] :]


def position():
    spot = lax.axis_index("gz")
    half = lax.axis_index("gy") & 1
    return spot, half, half * LINE + spot


def neighbours(h, spot, half, place):
    count = PAIR >> h
    q, low = place >> h, spot >> h
    return [
        (0, 0, jnp.maximum(q - 1, 0), q > 0),
        (0, 1, jnp.minimum(q + 1, count - 1), q < count - 1),
        (1, 0, count - 1, (half == 1) & (low == 0)),
        (1, 1, 0, (half == 0) & (low == (LINE >> h) - 1)),
    ]


def fold(up_ref, coup_ref, folded_ref, maps):
    spot, half, place = position()
    maps[TOPL][...] = jnp.zeros_like(maps[TOPL])
    down = [None]
    for h in range(1, TOPL + 1):
        step = up_ref[h - 1, (spot >> (h - 1)) & 1]
        down.append(step.T.astype(jnp.float32) if h == 1 else dot_wide(step, down[-1], TN))
    zero = jnp.zeros((RANK, RANK), jnp.float32)
    for h in range(TOPL, -1, -1):
        for to, side, q, used in neighbours(h, spot, half, place):
            mat = coup_ref[h, side]
            term = dot_wide(mat, down[h]) if h else mat.astype(jnp.float32)
            term = term * used.astype(jnp.float32)
            maps[h][q] += jnp.concatenate([zero, term] if to else [term, zero], 1)
        if h:
            mat = up_ref[h - 1].reshape(2 * RANK, RANK)
            for q in range(PAIR >> h):
                maps[h - 1][2 * q : 2 * q + 2] = dot_wide(mat, maps[h][q]).reshape(2, RANK, 2 * RANK)
    for j, (line, z) in enumerate(MEMBERS):
        values = maps[0][line * LINE + z]
        high = values.astype(jnp.bfloat16)
        at = slice(j * RANK, (j + 1) * RANK)
        folded_ref[0, at, :] = high
        folded_ref[1, at, :] = (values - high.astype(jnp.float32)).astype(jnp.bfloat16)


def hold(staged, kept, done):
    return [pltpu.make_async_copy(staged[i], kept[i], done.at[i]) for i in range(HELD)]


def levels_copies(up_hbm, coup_hbm, up_ref, coup_ref, done):
    return [
        pltpu.make_async_copy(up_hbm, up_ref, done.at[0]),
        pltpu.make_async_copy(coup_hbm, coup_ref, done.at[1]),
    ]


def coeff_kernel(*refs):
    count = STAGED + HELD
    staged, (up_hbm, coup_hbm), refs = refs[:count], refs[count : count + 2], refs[count + 2 :]
    coeffs_ref, sends_hbm, first_ref, second_ref, folded_ref = refs[:5]
    kept, (done, held, mats), refs = refs[5 : count + 5], refs[count + 5 : count + 8], refs[count + 8 :]
    up_ref, coup_ref, sends_ref, sent, maps = *refs[:4], refs[4:]
    spot = lax.axis_index("gz")
    early, folding = spot < EARLY, spot < FOLDED
    copies = [
        pltpu.make_async_copy(staged[i], kept[i], done.at[i]) for i in range(STAGED)
    ]
    for copy in copies:
        copy.start()

    @pl.when(early)
    def _():
        for copy in hold(staged[STAGED:], kept[STAGED:], held):
            copy.start()

    @pl.when(folding)
    def _():
        for copy in levels_copies(up_hbm, coup_hbm, up_ref, coup_ref, mats):
            copy.start()

    rhs_ref, basis_ref, transfer_ref = kept[:3]
    copies[0].wait()
    copies[1].wait()
    parts = []
    for t in range(LEAF_DEV):
        block = rhs_ref[:, t * LEAF : (t + 1) * LEAF]
        parts.append(dot(block, basis_ref[t], NT).astype(jnp.bfloat16))
    copies[2].wait()
    coeffs = jnp.concatenate(parts, 1)
    root = dot(coeffs, transfer_ref[...].reshape(LEAF_DEV * RANK, RANK))
    packed = jnp.concatenate([root[:8], root[8:]], 1)
    packed = jnp.concatenate([packed, packed], 0).astype(jnp.bfloat16)
    for j in range(PAIR // 2):
        sends_ref[16 * j : 16 * (j + 1), :] = packed
    sending = pltpu.make_async_copy(sends_ref, sends_hbm, sent.at[0])
    sending.start()
    coeffs_ref[...] = coeffs
    wide = REACH * LEAF
    tail = jnp.concatenate([rhs_ref[:, (LEAF_DEV - REACH) * LEAF :], coeffs[:, (LEAF_DEV - REACH) * RANK :]], 1)
    head = jnp.concatenate([rhs_ref[:, :wide], coeffs[:, : REACH * RANK]], 1)
    odd = jnp.broadcast_to(spot & 1, tail.shape) == 1
    first_ref[...] = jnp.where(odd, tail, head)
    second_ref[...] = jnp.where(odd, head, tail)
    for copy in copies[3:]:
        copy.wait()
    sending.wait()

    @pl.when(folding)
    def _():
        for copy in levels_copies(up_hbm, coup_hbm, up_ref, coup_ref, mats):
            copy.wait()
        fold(up_ref, coup_ref, folded_ref, maps)

    @pl.when(early)
    def _():
        for copy in hold(staged[STAGED:], kept[STAGED:], held):
            copy.wait()


def near_kernel(
    near_src, coup_src, rhs_ref, coeffs_ref, first_ref, second_ref, coupling_hbm, tiles_hbm,
    coupling_in, tiles_in, near_ref, field_ref, coupling_ref, tiles_ref, blocks, leaf_coeffs, held,
):
    late = lax.axis_index("gz") >= EARLY

    @pl.when(late)
    def _():
        for copy in hold([coupling_hbm, tiles_hbm], [coupling_ref, tiles_ref], held):
            copy.start()

    own = near_src[0, 0]
    anchor = own - REACH
    none = LEAF_DEV + 2 * REACH
    wide = REACH * LEAF
    above = REACH + LEAF_DEV
    odd = lax.axis_index("gz") & 1
    for side_ref, start in ((first_ref, above * odd), (second_ref, above * (1 - odd))):
        for i in range(REACH):
            blocks[start + i] = side_ref[:, i * LEAF : (i + 1) * LEAF]
            leaf_coeffs[start + i] = side_ref[:, wide + i * RANK : wide + (i + 1) * RANK]
    for t in range(LEAF_DEV):
        blocks[REACH + t] = rhs_ref[:, t * LEAF : (t + 1) * LEAF]
        leaf_coeffs[REACH + t] = coeffs_ref[:, t * RANK : (t + 1) * RANK]
    blocks[none] = jnp.zeros((NRHS, LEAF), jnp.bfloat16)
    leaf_coeffs[none] = jnp.zeros((NRHS, RANK), jnp.bfloat16)

    def place(source):
        return jnp.where(source >= 0, jnp.clip(source - anchor, 0, none - 1), none)

    @pl.when(late)
    def _():
        for copy in hold([coupling_hbm, tiles_hbm], [coupling_ref, tiles_ref], held):
            copy.wait()

    fields = []
    for t in range(LEAF_DEV):
        picked = jnp.concatenate([blocks[place(near_src[t, n])] for n in range(NEAR)], 1)
        near_ref[:, t * LEAF : (t + 1) * LEAF] = dot(picked, tiles_ref[t].reshape(NEAR * LEAF, LEAF))
        taken = jnp.concatenate([leaf_coeffs[place(coup_src[t, a])] for a in range(ADM)], 1)
        fields.append(dot(taken, coupling_ref[t].reshape(ADM * RANK, RANK)))
    field_ref[...] = jnp.concatenate(fields, 1)


def tree_kernel(got_ref, folded_ref, up_hbm, coup_hbm, own_ref, cross_ref, up_ref, coup_ref, mats, *levels):
    spot, half, place = position()
    wide = got_ref[...].astype(jnp.float32).reshape(PAIR, 8, 2 * RANK)

    @pl.when(spot < FOLDED)
    def _():
        parts = []
        for j in range(0, PAIR, 2):
            top = jnp.concatenate([wide[j, :, :RANK], wide[j + 1, :, :RANK]], 1)
            low = jnp.concatenate([wide[j, :, RANK:], wide[j + 1, :, RANK:]], 1)
            parts.append(jnp.concatenate([top, low], 0).astype(jnp.bfloat16))
        given = jnp.concatenate(parts, 1)
        both = dot(given, folded_ref[0]) + dot(given, folded_ref[1])
        own_ref[...] = both[:, :RANK]
        cross_ref[...] = jnp.concatenate([both[:8, RANK:], both[8:, RANK:]], 1)

    @pl.when(spot >= FOLDED)
    def _():
        copies = levels_copies(up_hbm, coup_hbm, up_ref, coup_ref, mats)
        for copy in copies:
            copy.start()
        for copy in copies:
            copy.wait()
        climb(wide, up_ref, coup_ref, own_ref, cross_ref, levels)


def climb(wide, up_ref, coup_ref, own_ref, cross_ref, levels):
    spot, half, place = position()
    for j, (line, z) in enumerate(MEMBERS):
        levels[0][0, line * LINE + z] = wide[j, :, :RANK]
        levels[0][1, line * LINE + z] = wide[j, :, RANK:]
    for h in range(1, TOPL + 1):
        count = PAIR >> h
        before = levels[h - 1][...].reshape(2, count, 2, 8, RANK)
        pairs = jnp.concatenate([before[:, :, 0], before[:, :, 1]], -1)
        mat = up_ref[h - 1].reshape(2 * RANK, RANK)
        levels[h][...] = dot_split(pairs.reshape(NRHS * count, 2 * RANK), mat).reshape(2, count, 8, RANK)

    fields = []
    for h in range(TOPL + 1):
        sides = [
            levels[h][:, q].reshape(NRHS, RANK) * used.astype(jnp.float32)
            for _, _, q, used in neighbours(h, spot, half, place)
        ]
        rows = jnp.concatenate([jnp.concatenate(sides[:2], 1), jnp.concatenate(sides[2:], 1)], 0)
        fields.append(dot_split(rows, coup_ref[h].reshape(2 * RANK, RANK)))
    incoming = fields[TOPL]
    for h in range(TOPL, 0, -1):
        parity = (spot >> (h - 1)) & 1
        incoming = fields[h - 1] + dot_split(incoming, up_ref[h - 1, parity], NT)
    own_ref[...] = incoming[:NRHS]
    cross_ref[...] = jnp.concatenate([incoming[NRHS : NRHS + 8], incoming[NRHS + 8 :]], 1)


def out_kernel(own_ref, cross_ref, field_ref, near_ref, transfer_ref, basis_ref, out_ref):
    cross = cross_ref[...]
    incoming = own_ref[...] + jnp.concatenate([cross[:, :RANK], cross[:, RANK:]], 0)
    spread = dot_split(incoming, transfer_ref[...].reshape(LEAF_DEV * RANK, RANK), NT)
    potential = (field_ref[...] + spread).astype(jnp.bfloat16)
    for t in range(LEAF_DEV):
        far = dot(potential[:, t * RANK : (t + 1) * RANK], basis_ref[t])
        at = slice(t * LEAF, (t + 1) * LEAF)
        out_ref[:, at] = (far + near_ref[:, at]).astype(jnp.bfloat16)


def crossed(values, count):
    route = []
    for line in range(1, count // LINE - 1, 2):
        for z in range(LINE):
            low = line * LINE + z
            route += [(low, low + LINE), (low + LINE, low)]
    return lax.ppermute(values, AXES, route)


def traded(values, count, odd):
    route = []
    for low in range(odd, count - 1, 2):
        route += [(low, low + 1), (low + 1, low)]
    return lax.ppermute(values, AXES, route)


def call(kernel, outs, scratch=(), ins=(), flops=0, moved=0, name=None, aliases=None, hbm=()):
    return pl.pallas_call(
        kernel,
        out_shape=[jax.ShapeDtypeStruct(shape, dtype) for shape, dtype in outs],
        in_specs=list(ins),
        out_specs=[HBM if i in hbm else VMEM for i in range(len(outs))],
        scratch_shapes=list(scratch),
        cost_estimate=pl.CostEstimate(flops=flops, bytes_accessed=moved, transcendentals=0),
        compiler_params=pltpu.CompilerParams(vmem_limit_bytes=24 * 2**20),
        input_output_aliases=aliases or {},
        name=name,
    )


def local(
    rhs,
    leaf_basis,
    leaf_transfer,
    leaf_coupling,
    coupling_sources,
    near_tiles,
    near_sources,
    top_transfer,
    cluster_coupling,
):
    bf16, f32 = jnp.bfloat16, jnp.float32
    count = lax.axis_size(AXES)
    width = LEAF_DEV * LEAF
    ranks = LEAF_DEV * RANK
    inputs = (
        rhs, leaf_basis, leaf_transfer, near_sources, coupling_sources,
        leaf_coupling, near_tiles, top_transfer, cluster_coupling,
    )
    inputs = [pltpu.with_memory_space_constraint(x, pltpu.HBM) for x in inputs]
    coeffs, sends, first, second, folded, *kept = call(
        coeff_kernel,
        [
            ((NRHS, ranks), bf16),
            ((PAIR * 8, 2 * RANK), bf16),
            ((NRHS, EDGE), bf16),
            ((NRHS, EDGE), bf16),
            ((2, PAIR * RANK, 2 * RANK), bf16),
        ]
        + [(x.shape, x.dtype) for x in inputs[:-2]],
        scratch=[pltpu.SemaphoreType.DMA((n,)) for n in (STAGED, HELD, 2)]
        + [pltpu.VMEM(x.shape, bf16) for x in inputs[-2:]]
        + [pltpu.VMEM((PAIR * 8, 2 * RANK), bf16), pltpu.SemaphoreType.DMA((1,))]
        + [pltpu.VMEM((PAIR >> h, RANK, 2 * RANK), f32) for h in range(TOPL + 1)],
        ins=[HBM] * len(inputs),
        hbm=[1],
        flops=2 * NRHS * ranks * (LEAF + RANK),
        moved=2**21,
        name="coeffs",
    )(*inputs)
    rhs, leaf_basis, leaf_transfer, near_sources, coupling_sources = kept[:STAGED]
    coupling_kept, tiles_kept = kept[STAGED:]
    pairs = [
        [(2 * k + line) * LINE + z for line, z in MEMBERS]
        for k in range(lax.axis_size("gy") // 2)
    ]
    got = lax.all_to_all(sends, ("gy", "gz"), 0, 0, tiled=True, axis_index_groups=pairs)
    first = traded(first, count, 1)
    second = traded(second, count, 0)
    near, field, _, _ = call(
        near_kernel,
        [((NRHS, width), f32), ((NRHS, ranks), f32)]
        + [(x.shape, x.dtype) for x in (coupling_kept, tiles_kept)],
        scratch=[
            pltpu.VMEM((LEAF_DEV + 2 * REACH + 1, NRHS, LEAF), bf16),
            pltpu.VMEM((LEAF_DEV + 2 * REACH + 1, NRHS, RANK), bf16),
            pltpu.SemaphoreType.DMA((HELD,)),
        ],
        ins=[SMEM, SMEM] + [VMEM] * 4 + [HBM] * 2 + [VMEM] * 2,
        aliases={8: 2, 9: 3},
        flops=2 * NRHS * LEAF_DEV * (NEAR * LEAF * LEAF + ADM * RANK * RANK),
        moved=2**21,
        name="near",
    )(near_sources, coupling_sources, rhs, coeffs, first, second, *inputs[STAGED:-2], coupling_kept, tiles_kept)
    own, cross = call(
        tree_kernel,
        [((NRHS, RANK), f32), ((8, 2 * RANK), f32)],
        scratch=[pltpu.VMEM(x.shape, bf16) for x in inputs[-2:]]
        + [pltpu.SemaphoreType.DMA((2,))]
        + [pltpu.VMEM((2, PAIR >> h, 8, RANK), f32) for h in range(TOPL + 1)],
        ins=[VMEM] * 2 + [HBM] * 2,
        flops=2**23,
        moved=2**18,
        name="tree",
    )(got, folded, *inputs[-2:])
    cross = crossed(cross, count)
    return call(
        out_kernel,
        [((NRHS, width), bf16)],
        ins=[VMEM] * 6,
        flops=2 * NRHS * ranks * (LEAF + RANK),
        moved=2**18,
        name="out",
    )(own, cross, field, near, leaf_transfer, leaf_basis)[0]


def solution(mesh):
    placed = (
        P(None, AXES),
        P(AXES, None, None),
        P(AXES, None, None),
        P(AXES, None, None, None),
        P(AXES, None),
        P(AXES, None, None, None),
        P(AXES, None),
        P(),
        P(),
    )
    return jax.shard_map(
        local, mesh=mesh, in_specs=placed, out_specs=P(None, AXES), check_vma=False
    )
```

```python
import jax
import jax.numpy as jnp
from jax import lax
from jax.experimental import pallas as pl
from jax.experimental.pallas import tpu as pltpu
from jax.sharding import PartitionSpec as P

LEAF = 256
RANK = 64
NRHS = 16
NEAR = 3
ADM = 6
TOPL = 4
LEAF_DEV = 4
REACH = 2
LINE = 16
PAIR = 2 * LINE
LEADER = 11
MEMBERS = [(1, LEADER)] + [(line, z) for line in (0, 1) for z in [12, 11, 10, 9, 8, 7, 6, 5, 4, 3, 2, 1, 0, 15, 14, 13] if (line, z) != (1, LEADER)]
AXES = ("gx", "gy", "gz")
EDGE = REACH * (LEAF + RANK)
VMEM = pl.BlockSpec(memory_space=pltpu.VMEM)
SMEM = pl.BlockSpec(memory_space=pltpu.SMEM)
HBM = pl.BlockSpec(memory_space=pltpu.HBM)
STAGED = 5
HELD = 2
EARLY = 6
FOLDED = 3
NT = (((1,), (1,)), ((), ()))
NN = (((1,), (0,)), ((), ()))
TN = (((0,), (0,)), ((), ()))


def dot(a, b, dims=NN):
    return lax.dot_general(a, b, dims, preferred_element_type=jnp.float32)


def dot_split(a, b, dims=NN):
    high = a.astype(jnp.bfloat16)
    low = (a - high.astype(jnp.float32)).astype(jnp.bfloat16)
    both = dot(jnp.concatenate([high, low], 0), b, dims)
    return both[: a.shape[0]] + both[a.shape[0] :]


def dot_wide(a, b, dims=NN):
    high = b.astype(jnp.bfloat16)
    low = (b - high.astype(jnp.float32)).astype(jnp.bfloat16)
    both = dot(a, jnp.concatenate([high, low], 1), dims)
    return both[:, : b.shape[1]] + both[:, b.shape[1] :]


def position():
    spot = lax.axis_index("gz")
    half = lax.axis_index("gy") & 1
    return spot, half, half * LINE + spot


def neighbours(h, spot, half, place):
    count = PAIR >> h
    q, low = place >> h, spot >> h
    return [
        (0, 0, jnp.maximum(q - 1, 0), q > 0),
        (0, 1, jnp.minimum(q + 1, count - 1), q < count - 1),
        (1, 0, count - 1, (half == 1) & (low == 0)),
        (1, 1, 0, (half == 0) & (low == (LINE >> h) - 1)),
    ]


def fold(up_ref, coup_ref, folded_ref, maps):
    spot, half, place = position()
    maps[TOPL][...] = jnp.zeros_like(maps[TOPL])
    down = [None]
    for h in range(1, TOPL + 1):
        step = up_ref[h - 1, (spot >> (h - 1)) & 1]
        down.append(step.T.astype(jnp.float32) if h == 1 else dot_wide(step, down[-1], TN))
    zero = jnp.zeros((RANK, RANK), jnp.float32)
    for h in range(TOPL, -1, -1):
        for to, side, q, used in neighbours(h, spot, half, place):
            mat = coup_ref[h, side]
            term = dot_wide(mat, down[h]) if h else mat.astype(jnp.float32)
            term = term * used.astype(jnp.float32)
            maps[h][q] += jnp.concatenate([zero, term] if to else [term, zero], 1)
        if h:
            mat = up_ref[h - 1].reshape(2 * RANK, RANK)
            for q in range(PAIR >> h):
                maps[h - 1][2 * q : 2 * q + 2] = dot_wide(mat, maps[h][q]).reshape(2, RANK, 2 * RANK)
    for j, (line, z) in enumerate(MEMBERS):
        values = maps[0][line * LINE + z]
        high = values.astype(jnp.bfloat16)
        at = slice(j * RANK, (j + 1) * RANK)
        folded_ref[0, at, :] = high
        folded_ref[1, at, :] = (values - high.astype(jnp.float32)).astype(jnp.bfloat16)


def hold(staged, kept, done):
    return [pltpu.make_async_copy(staged[i], kept[i], done.at[i]) for i in range(HELD)]


def levels_copies(up_hbm, coup_hbm, up_ref, coup_ref, done):
    return [
        pltpu.make_async_copy(up_hbm, up_ref, done.at[0]),
        pltpu.make_async_copy(coup_hbm, coup_ref, done.at[1]),
    ]


def coeff_kernel(*refs):
    count = STAGED + HELD
    staged, (up_hbm, coup_hbm), refs = refs[:count], refs[count : count + 2], refs[count + 2 :]
    coeffs_ref, sends_hbm, first_ref, second_ref, folded_ref = refs[:5]
    kept, (done, held, mats), refs = refs[5 : count + 5], refs[count + 5 : count + 8], refs[count + 8 :]
    up_ref, coup_ref, sends_ref, sent, maps = *refs[:4], refs[4:]
    spot = lax.axis_index("gz")
    early, folding = spot < EARLY, spot < FOLDED
    copies = [
        pltpu.make_async_copy(staged[i], kept[i], done.at[i]) for i in range(STAGED)
    ]
    for copy in copies:
        copy.start()

    @pl.when(early)
    def _():
        for copy in hold(staged[STAGED:], kept[STAGED:], held):
            copy.start()

    @pl.when(folding)
    def _():
        for copy in levels_copies(up_hbm, coup_hbm, up_ref, coup_ref, mats):
            copy.start()

    rhs_ref, basis_ref, transfer_ref = kept[:3]
    copies[0].wait()
    copies[1].wait()
    parts = []
    for t in range(LEAF_DEV):
        block = rhs_ref[:, t * LEAF : (t + 1) * LEAF]
        parts.append(dot(block, basis_ref[t], NT).astype(jnp.bfloat16))
    copies[2].wait()
    coeffs = jnp.concatenate(parts, 1)
    root = dot(coeffs, transfer_ref[...].reshape(LEAF_DEV * RANK, RANK))
    packed = jnp.concatenate([root[:8], root[8:]], 1)
    packed = jnp.concatenate([packed, packed], 0).astype(jnp.bfloat16)
    for j in range(PAIR // 2):
        sends_ref[16 * j : 16 * (j + 1), :] = packed
    sending = pltpu.make_async_copy(sends_ref, sends_hbm, sent.at[0])
    sending.start()
    coeffs_ref[...] = coeffs
    wide = REACH * LEAF
    tail = jnp.concatenate([rhs_ref[:, (LEAF_DEV - REACH) * LEAF :], coeffs[:, (LEAF_DEV - REACH) * RANK :]], 1)
    head = jnp.concatenate([rhs_ref[:, :wide], coeffs[:, : REACH * RANK]], 1)
    odd = jnp.broadcast_to(spot & 1, tail.shape) == 1
    first_ref[...] = jnp.where(odd, tail, head)
    second_ref[...] = jnp.where(odd, head, tail)
    for copy in copies[3:]:
        copy.wait()
    sending.wait()

    @pl.when(folding)
    def _():
        for copy in levels_copies(up_hbm, coup_hbm, up_ref, coup_ref, mats):
            copy.wait()
        fold(up_ref, coup_ref, folded_ref, maps)

    @pl.when(early)
    def _():
        for copy in hold(staged[STAGED:], kept[STAGED:], held):
            copy.wait()


def near_kernel(
    near_src, coup_src, rhs_ref, coeffs_ref, first_ref, second_ref, coupling_hbm, tiles_hbm,
    coupling_in, tiles_in, near_ref, field_ref, coupling_ref, tiles_ref, blocks, leaf_coeffs, held,
):
    late = lax.axis_index("gz") >= EARLY

    @pl.when(late)
    def _():
        for copy in hold([coupling_hbm, tiles_hbm], [coupling_ref, tiles_ref], held):
            copy.start()

    own = near_src[0, 0]
    anchor = own - REACH
    none = LEAF_DEV + 2 * REACH
    wide = REACH * LEAF
    above = REACH + LEAF_DEV
    odd = lax.axis_index("gz") & 1
    for side_ref, start in ((first_ref, above * odd), (second_ref, above * (1 - odd))):
        for i in range(REACH):
            blocks[start + i] = side_ref[:, i * LEAF : (i + 1) * LEAF]
            leaf_coeffs[start + i] = side_ref[:, wide + i * RANK : wide + (i + 1) * RANK]
    for t in range(LEAF_DEV):
        blocks[REACH + t] = rhs_ref[:, t * LEAF : (t + 1) * LEAF]
        leaf_coeffs[REACH + t] = coeffs_ref[:, t * RANK : (t + 1) * RANK]
    blocks[none] = jnp.zeros((NRHS, LEAF), jnp.bfloat16)
    leaf_coeffs[none] = jnp.zeros((NRHS, RANK), jnp.bfloat16)

    def place(source):
        return jnp.where(source >= 0, jnp.clip(source - anchor, 0, none - 1), none)

    @pl.when(late)
    def _():
        for copy in hold([coupling_hbm, tiles_hbm], [coupling_ref, tiles_ref], held):
            copy.wait()

    fields = []
    for t in range(LEAF_DEV):
        picked = jnp.concatenate([blocks[place(near_src[t, n])] for n in range(NEAR)], 1)
        near_ref[:, t * LEAF : (t + 1) * LEAF] = dot(picked, tiles_ref[t].reshape(NEAR * LEAF, LEAF))
        taken = jnp.concatenate([leaf_coeffs[place(coup_src[t, a])] for a in range(ADM)], 1)
        fields.append(dot(taken, coupling_ref[t].reshape(ADM * RANK, RANK)))
    field_ref[...] = jnp.concatenate(fields, 1)


def tree_kernel(got_ref, folded_ref, up_hbm, coup_hbm, own_ref, cross_ref, up_ref, coup_ref, mats, *levels):
    spot, half, place = position()
    wide = got_ref[...].astype(jnp.float32).reshape(PAIR, 8, 2 * RANK)

    @pl.when(spot < FOLDED)
    def _():
        parts = []
        for j in range(0, PAIR, 2):
            top = jnp.concatenate([wide[j, :, :RANK], wide[j + 1, :, :RANK]], 1)
            low = jnp.concatenate([wide[j, :, RANK:], wide[j + 1, :, RANK:]], 1)
            parts.append(jnp.concatenate([top, low], 0).astype(jnp.bfloat16))
        given = jnp.concatenate(parts, 1)
        both = dot(given, folded_ref[0]) + dot(given, folded_ref[1])
        own_ref[...] = both[:, :RANK]
        cross_ref[...] = jnp.concatenate([both[:8, RANK:], both[8:, RANK:]], 1)

    @pl.when(spot >= FOLDED)
    def _():
        copies = levels_copies(up_hbm, coup_hbm, up_ref, coup_ref, mats)
        for copy in copies:
            copy.start()
        for copy in copies:
            copy.wait()
        climb(wide, up_ref, coup_ref, own_ref, cross_ref, levels)


def climb(wide, up_ref, coup_ref, own_ref, cross_ref, levels):
    spot, half, place = position()
    for j, (line, z) in enumerate(MEMBERS):
        levels[0][0, line * LINE + z] = wide[j, :, :RANK]
        levels[0][1, line * LINE + z] = wide[j, :, RANK:]
    for h in range(1, TOPL + 1):
        count = PAIR >> h
        before = levels[h - 1][...].reshape(2, count, 2, 8, RANK)
        pairs = jnp.concatenate([before[:, :, 0], before[:, :, 1]], -1)
        mat = up_ref[h - 1].reshape(2 * RANK, RANK)
        levels[h][...] = dot_split(pairs.reshape(NRHS * count, 2 * RANK), mat).reshape(2, count, 8, RANK)

    fields = []
    for h in range(TOPL + 1):
        sides = [
            levels[h][:, q].reshape(NRHS, RANK) * used.astype(jnp.float32)
            for _, _, q, used in neighbours(h, spot, half, place)
        ]
        rows = jnp.concatenate([jnp.concatenate(sides[:2], 1), jnp.concatenate(sides[2:], 1)], 0)
        fields.append(dot_split(rows, coup_ref[h].reshape(2 * RANK, RANK)))
    incoming = fields[TOPL]
    for h in range(TOPL, 0, -1):
        parity = (spot >> (h - 1)) & 1
        incoming = fields[h - 1] + dot_split(incoming, up_ref[h - 1, parity], NT)
    own_ref[...] = incoming[:NRHS]
    cross_ref[...] = jnp.concatenate([incoming[NRHS : NRHS + 8], incoming[NRHS + 8 :]], 1)


def out_kernel(own_ref, cross_ref, field_ref, near_ref, transfer_ref, basis_ref, out_ref):
    cross = cross_ref[...]
    incoming = own_ref[...] + jnp.concatenate([cross[:, :RANK], cross[:, RANK:]], 0)
    spread = dot_split(incoming, transfer_ref[...].reshape(LEAF_DEV * RANK, RANK), NT)
    potential = (field_ref[...] + spread).astype(jnp.bfloat16)
    for t in range(LEAF_DEV):
        far = dot(potential[:, t * RANK : (t + 1) * RANK], basis_ref[t])
        at = slice(t * LEAF, (t + 1) * LEAF)
        out_ref[:, at] = (far + near_ref[:, at]).astype(jnp.bfloat16)


def crossed(values, count):
    route = []
    for line in range(1, count // LINE - 1, 2):
        for z in range(LINE):
            low = line * LINE + z
            route += [(low, low + LINE), (low + LINE, low)]
    return lax.ppermute(values, AXES, route)


def traded(values, count, odd):
    route = []
    for low in range(odd, count - 1, 2):
        route += [(low, low + 1), (low + 1, low)]
    return lax.ppermute(values, AXES, route)


def call(kernel, outs, scratch=(), ins=(), flops=0, moved=0, name=None, aliases=None, hbm=()):
    return pl.pallas_call(
        kernel,
        out_shape=[jax.ShapeDtypeStruct(shape, dtype) for shape, dtype in outs],
        in_specs=list(ins),
        out_specs=[HBM if i in hbm else VMEM for i in range(len(outs))],
        scratch_shapes=list(scratch),
        cost_estimate=pl.CostEstimate(flops=flops, bytes_accessed=moved, transcendentals=0),
        compiler_params=pltpu.CompilerParams(vmem_limit_bytes=24 * 2**20),
        input_output_aliases=aliases or {},
        name=name,
    )


def local(
    rhs,
    leaf_basis,
    leaf_transfer,
    leaf_coupling,
    coupling_sources,
    near_tiles,
    near_sources,
    top_transfer,
    cluster_coupling,
):
    bf16, f32 = jnp.bfloat16, jnp.float32
    count = lax.axis_size(AXES)
    width = LEAF_DEV * LEAF
    ranks = LEAF_DEV * RANK
    inputs = (
        rhs, leaf_basis, leaf_transfer, near_sources, coupling_sources,
        leaf_coupling, near_tiles, top_transfer, cluster_coupling,
    )
    inputs = [pltpu.with_memory_space_constraint(x, pltpu.HBM) for x in inputs]
    coeffs, sends, first, second, folded, *kept = call(
        coeff_kernel,
        [
            ((NRHS, ranks), bf16),
            ((PAIR * 8, 2 * RANK), bf16),
            ((NRHS, EDGE), bf16),
            ((NRHS, EDGE), bf16),
            ((2, PAIR * RANK, 2 * RANK), bf16),
        ]
        + [(x.shape, x.dtype) for x in inputs[:-2]],
        scratch=[pltpu.SemaphoreType.DMA((n,)) for n in (STAGED, HELD, 2)]
        + [pltpu.VMEM(x.shape, bf16) for x in inputs[-2:]]
        + [pltpu.VMEM((PAIR * 8, 2 * RANK), bf16), pltpu.SemaphoreType.DMA((1,))]
        + [pltpu.VMEM((PAIR >> h, RANK, 2 * RANK), f32) for h in range(TOPL + 1)],
        ins=[HBM] * len(inputs),
        hbm=[1],
        flops=2 * NRHS * ranks * (LEAF + RANK),
        moved=2**21,
        name="coeffs",
    )(*inputs)
    rhs, leaf_basis, leaf_transfer, near_sources, coupling_sources = kept[:STAGED]
    coupling_kept, tiles_kept = kept[STAGED:]
    pairs = [
        [(2 * k + line) * LINE + z for line, z in MEMBERS]
        for k in range(lax.axis_size("gy") // 2)
    ]
    got = lax.all_to_all(sends, ("gy", "gz"), 0, 0, tiled=True, axis_index_groups=pairs)
    first = traded(first, count, 1)
    second = traded(second, count, 0)
    near, field, _, _ = call(
        near_kernel,
        [((NRHS, width), f32), ((NRHS, ranks), f32)]
        + [(x.shape, x.dtype) for x in (coupling_kept, tiles_kept)],
        scratch=[
            pltpu.VMEM((LEAF_DEV + 2 * REACH + 1, NRHS, LEAF), bf16),
            pltpu.VMEM((LEAF_DEV + 2 * REACH + 1, NRHS, RANK), bf16),
            pltpu.SemaphoreType.DMA((HELD,)),
        ],
        ins=[SMEM, SMEM] + [VMEM] * 4 + [HBM] * 2 + [VMEM] * 2,
        aliases={8: 2, 9: 3},
        flops=2 * NRHS * LEAF_DEV * (NEAR * LEAF * LEAF + ADM * RANK * RANK),
        moved=2**21,
        name="near",
    )(near_sources, coupling_sources, rhs, coeffs, first, second, *inputs[STAGED:-2], coupling_kept, tiles_kept)
    own, cross = call(
        tree_kernel,
        [((NRHS, RANK), f32), ((8, 2 * RANK), f32)],
        scratch=[pltpu.VMEM(x.shape, bf16) for x in inputs[-2:]]
        + [pltpu.SemaphoreType.DMA((2,))]
        + [pltpu.VMEM((2, PAIR >> h, 8, RANK), f32) for h in range(TOPL + 1)],
        ins=[VMEM] * 2 + [HBM] * 2,
        flops=2**23,
        moved=2**18,
        name="tree",
    )(got, folded, *inputs[-2:])
    cross = crossed(cross, count)
    return call(
        out_kernel,
        [((NRHS, width), bf16)],
        ins=[VMEM] * 6,
        flops=2 * NRHS * ranks * (LEAF + RANK),
        moved=2**18,
        name="out",
    )(own, cross, field, near, leaf_transfer, leaf_basis)[0]


def solution(mesh):
    placed = (
        P(None, AXES),
        P(AXES, None, None),
        P(AXES, None, None),
        P(AXES, None, None, None),
        P(AXES, None),
        P(AXES, None, None, None),
        P(AXES, None),
        P(),
        P(),
    )
    return jax.shard_map(
        local, mesh=mesh, in_specs=placed, out_specs=P(None, AXES), check_vma=False
    )
```
